128 devices in a mesh: narrow: 4 (over y_hi, core), wide: 32 (over z, y_lo, x).
Axes of the slice: x: 4, y: 4 (y_hi: 2, y_lo: 2; y = y_hi * 2 + y_lo), z: 4, core: 2. Of those that a mesh axis runs over, the one named last changes fastest.
Arguments:
- velocity: float32 [3, 384, 512, 512], P(None, None, 'wide', 'narrow'), may hold values from -6 to 6
- inv_spacing: float32 [384], replicated, may hold values from 0.5 to 2
- eigen_wall: float32 [384], P(('narrow', 'wide')), may hold values from 0.01 to 1
- to_modes: float32 [384, 384], replicated, may hold values from -1 to 2
- from_modes: float32 [384, 384], replicated, may hold values from -1 to 2
Outputs:
- new_velocity: float32 [3, 384, 512, 512], P(None, None, 'wide', 'narrow')
The draws below stay inside these ranges and needn't reach their ends.
All inputs are finite; a program needn't handle non-finite values.
Results may differ from the reference program's by a relative error of at most 0.035.
Values sent between devices are 32-bit elements; how exact they have to be, the bound alone decides.
A program may use at most 192 MiB of HBM per device.

```python
import math
import jax
import jax.numpy as jnp
from jax import lax

NX = 512
NY = 384
NZ = 512


def mode_matrix(key):
    noise = jnp.clip(jax.random.normal(key, (NY, NY), jnp.float32), -4.0, 4.0)
    return jnp.eye(NY, dtype=jnp.float32) + 0.5 * noise / jnp.sqrt(jnp.float32(NY))


def draw_to_modes(key, part):
    key = jax.random.fold_in(key, 11)
    return mode_matrix(key)


def draw_from_modes(key, part):
    key = jax.random.fold_in(key, 23)
    return mode_matrix(key)


def draw_eigen_wall(key, part):
    key = jax.random.fold_in(key, 37)
    spread = jax.random.uniform(key, (NY,), jnp.float32, 0.0, 1.0)
    return (0.01 * jnp.power(jnp.float32(100.0), spread)).astype(jnp.float32)


def block_levels(stream_key, dims, split, smallest, largest):
    def one(dim, parts):
        draws = jax.random.uniform(jax.random.fold_in(jax.random.fold_in(stream_key, 6), dim), (parts,), jnp.float32, smallest / len(split), largest / len(split))
        return jnp.repeat(jnp.exp(draws), dims[dim] // parts).reshape((-1,) + (1,) * (len(dims) - dim - 1))

    loudness = one(*split[0])
    for cut in split[1:]:
        loudness = loudness * one(*cut)
    return loudness


def centred(rng, dims, width, bound, pieces=(), held_as=jnp.bfloat16):
    result = jax.random.normal(rng, dims, jnp.float32) * width
    if len(pieces) > 0:
        result = block_levels(rng, dims, pieces, -0.22, 0.18) * result
    return jnp.clip(result, min=-bound, max=bound).astype(held_as)


def setup_inputs(seed: int = 0) -> dict:
    arg_keys = jax.random.split(jax.random.key(seed), 6)
    return {
        "velocity": centred(arg_keys[0], (3, NY, NZ, NX), 1.0, 6.0, ((2, 32), (3, 4)), jnp.float32),
        "inv_spacing": jnp.clip(jnp.exp(jax.random.uniform(arg_keys[1], (NY,), jnp.float32, math.log(0.5), math.log(2.0))), 0.5, 2.0),
        "eigen_wall": draw_eigen_wall(jax.random.fold_in(arg_keys[5], 71), 0),
        "to_modes": draw_to_modes(jax.random.fold_in(arg_keys[5], 71), 0),
        "from_modes": draw_from_modes(jax.random.fold_in(arg_keys[5], 71), 0),
    }


time_step = 0.1
viscosity = 0.5

def fourier_table(length):
    row_index = jnp.arange(length, dtype=jnp.int32)[:, None]
    col_index = jnp.arange(length, dtype=jnp.int32)[None, :]
    middle = length // 2
    wavenum = jnp.where(row_index <= middle, row_index, row_index - middle)
    phase = (wavenum * col_index % length).astype(jnp.float32) * (2.0 * math.pi / length)
    waves = jnp.where(row_index <= middle, jnp.cos(phase), jnp.sin(phase))
    weight = jnp.where((row_index == 0) | (row_index == middle), math.sqrt(1.0 / length), math.sqrt(2.0 / length))
    eigen = 2.0 - 2.0 * jnp.cos(wavenum[:, 0].astype(jnp.float32) * (2.0 * math.pi / length))
    return ((waves * weight).astype(jnp.float32), eigen.astype(jnp.float32))

def wall_terms(field, inv_spacing):
    zero = jnp.zeros_like(field[..., :1, :, :])
    upper = jnp.concatenate([field[..., 1:, :, :], zero], axis=-3)
    lower = jnp.concatenate([zero, field[..., :-1, :, :]], axis=-3)
    scale = inv_spacing[:, None, None]
    return ((upper - lower) * 0.5 * scale, (upper - 2.0 * field + lower) * scale * scale)

def predict(extended, inv_spacing):
    centre = extended[:, :, 1:-1, 1:-1]
    east = extended[:, :, 1:-1, 2:]
    west = extended[:, :, 1:-1, :-2]
    north = extended[:, :, 2:, 1:-1]
    south = extended[:, :, :-2, 1:-1]
    grad_wall, curve_wall = wall_terms(centre, inv_spacing)
    laplace = east + west - 2.0 * centre + (north + south - 2.0 * centre) + curve_wall
    advect = centre[0] * ((east - west) * 0.5) + centre[1] * grad_wall + centre[2] * ((north - south) * 0.5)
    return centre + time_step * (viscosity * laplace - advect)

def diverge(extended, inv_spacing):
    stream = (extended[0, :, 1:-1, 2:] - extended[0, :, 1:-1, :-2]) * 0.5
    normal = wall_terms(extended[1, :, 1:-1, 1:-1], inv_spacing)[0]
    span = (extended[2, :, 2:, 1:-1] - extended[2, :, :-2, 1:-1]) * 0.5
    return (stream + normal + span) / time_step

def correct(star, press_ext, inv_spacing):
    press = press_ext[0]
    centre = press[:, 1:-1, 1:-1]
    grad_x = (press[:, 1:-1, 2:] - press[:, 1:-1, :-2]) * 0.5
    grad_y = wall_terms(centre, inv_spacing)[0]
    grad_z = (press[:, 2:, 1:-1] - press[:, :-2, 1:-1]) * 0.5
    return star - time_step * jnp.stack([grad_x, grad_y, grad_z])

def wrap_pad(field):
    return jnp.pad(field, ((0, 0), (0, 0), (1, 1), (1, 1)), mode='wrap')

def reference(velocity, inv_spacing, eigen_wall, to_modes, from_modes):
    highest = lax.Precision.HIGHEST
    table_x, eigen_x = fourier_table(NX)
    table_z, eigen_z = fourier_table(NZ)
    star = predict(wrap_pad(velocity), inv_spacing)
    source = diverge(wrap_pad(star), inv_spacing)
    modal = jnp.einsum('my,yzx->mzx', to_modes, source, precision=highest)
    spectra = jnp.einsum('kx,mzx->mzk', table_x, modal, precision=highest)
    spectra = jnp.einsum('qz,mzk->mqk', table_z, spectra, precision=highest)
    solved = -spectra / (eigen_wall[:, None, None] + eigen_z[None, :, None] + eigen_x[None, None, :])
    physical = jnp.einsum('qz,mqk->mzk', table_z, solved, precision=highest)
    physical = jnp.einsum('kx,mzk->mzx', table_x, physical, precision=highest)
    pressure = jnp.einsum('ym,mzx->yzx', from_modes, physical, precision=highest)
    return correct(star, wrap_pad(pressure[None]), inv_spacing)
```

```python
import functools
import math

import jax
import numpy as np
import jax.numpy as jnp
from jax import lax
from jax.sharding import PartitionSpec as P

NX = 512
NZ = 512


time_step = 0.1
viscosity = 0.5


def extended_2(shard, sides, width):
    for axis, dim in sides:
        peers, length = (lax.axis_size(axis), shard.shape[dim])
        up = [(i, (i + 1) % peers) for i in range(peers)]
        down = [(j, i) for i, j in up]
        last = lax.slice_in_dim(shard, length - width, length, axis=dim)
        leading = lax.slice_in_dim(shard, 0, width, axis=dim)
        before = lax.ppermute(last, axis, up)
        after = lax.ppermute(leading, axis, down)
        shard = jnp.concatenate([before, shard, after], axis=dim)
    return shard


def wall_terms(field, inv_spacing):
    zero = jnp.zeros_like(field[..., :1, :, :])
    upper = jnp.concatenate([field[..., 1:, :, :], zero], axis=-3)
    lower = jnp.concatenate([zero, field[..., :-1, :, :]], axis=-3)
    scale = inv_spacing[:, None, None]
    return ((upper - lower) * 0.5 * scale, (upper - 2.0 * field + lower) * scale * scale)


def predict(extended, inv_spacing):
    centre = extended[:, :, 1:-1, 1:-1]
    east = extended[:, :, 1:-1, 2:]
    west = extended[:, :, 1:-1, :-2]
    north = extended[:, :, 2:, 1:-1]
    south = extended[:, :, :-2, 1:-1]
    grad_wall, curve_wall = wall_terms(centre, inv_spacing)
    laplace = east + west - 2.0 * centre + (north + south - 2.0 * centre) + curve_wall
    advect = (
        centre[0] * ((east - west) * 0.5)
        + centre[1] * grad_wall
        + centre[2] * ((north - south) * 0.5)
    )
    return centre + time_step * (viscosity * laplace - advect)


def diverge(extended, inv_spacing):
    stream = (extended[0, :, 1:-1, 2:] - extended[0, :, 1:-1, :-2]) * 0.5
    normal = wall_terms(extended[1, :, 1:-1, 1:-1], inv_spacing)[0]
    span = (extended[2, :, 2:, 1:-1] - extended[2, :, :-2, 1:-1]) * 0.5
    return (stream + normal + span) / time_step


def cosines(n):
    j = np.arange(n)[:, None]; z = np.arange(n)[None, :]
    q = np.cos(np.pi * j * (z + 0.5) / n) * np.where(j == 0, math.sqrt(1 / n), math.sqrt(2 / n))
    return q, 2 - 2 * np.cos(np.pi * np.arange(n) / n)

def fourier(n):
    r = np.arange(n)[:, None]; c = np.arange(n)[None, :]
    mid = n // 2
    k = np.where(r <= mid, r, r - mid)
    ph = (k * c % n) * (2 * np.pi / n)
    w = np.where(r <= mid, np.cos(ph), np.sin(ph))
    s = np.where((r == 0) | (r == mid), math.sqrt(1 / n), math.sqrt(2 / n))
    return w * s, 2 - 2 * np.cos(2 * np.pi * k[:, 0] / n)

prec = lax.Precision.HIGH
ein = functools.partial(jnp.einsum, precision=prec)
f32 = lambda a: jnp.asarray(np.asarray(a, np.float32))

def solve(modal, c_all, c_own, nb, nn):
    M, lz, lx = modal.shape
    ND = nb * nn
    R = M // ND
    Qz, nu = cosines(lz); Qx, mu = cosines(lx)
    qLz, qFz = Qz[:, -1], Qz[:, 0]; qLx, qFx = Qx[:, -1], Qx[:, 0]
    lam = c_all[None, :, None] + f32(nu)[:, None, None] + f32(mu)[None, None, :]
    fh = ein("jz,ix,mzx->jmi", f32(Qz), f32(Qx), modal)
    gh = fh / lam
    zl = ein("j,jmi->mi", f32(qLz), gh); zf = ein("j,jmi->mi", f32(qFz), gh)
    xl = ein("i,jmi->mj", f32(qLx), gh); xf = ein("i,jmi->mj", f32(qFx), gh)
    send = jnp.concatenate([zl, zf, xl, xf], axis=1).reshape(R, ND, -1).transpose(1, 0, 2)
    recv = lax.all_to_all(send, ("narrow", "wide"), split_axis=0, concat_axis=0, tiled=True)
    recv = recv.reshape(nn, nb, R, -1)
    zl, zf, xl, xf = jnp.split(recv, [lx, 2 * lx, 2 * lx + lz], axis=-1)
    up = lambda a: jnp.roll(a, -1, axis=1)
    dn = lambda a: jnp.roll(a, 1, axis=1)
    ea = lambda a: jnp.roll(a, -1, axis=0)
    we = lambda a: jnp.roll(a, 1, axis=0)
    aW = zl - up(zf)
    aV = xl - ea(xf)
    D = 1.0 / (c_own[:, None, None] + f32(nu)[None, :, None] + f32(mu)[None, None, :])
    hll = ein("rji,i->rj", D, f32(qLx * qLx)); hlf = ein("rji,i->rj", D, f32(qLx * qFx))
    Fn, en = fourier(nn)
    lamn = 1 + 2 * hll[..., None] - 2 * hlf[..., None] * f32(1 - en / 2)
    def SVinv(a):
        t = ein("en,nbrj->ebrj", f32(Fn), a)
        t = t / lamn.transpose(2, 0, 1)[:, None]
        return ein("en,ebrj->nbrj", f32(Fn), t)
    t = SVinv(aV)
    T = f32(qLz) * t - f32(qFz) * up(t)
    TD = ein("nbrj,rji->nbri", T, D)
    aW = aW - (f32(qLx) * TD - f32(qFx) * we(TD))
    Bx, ex = fourier(nn * lx)
    Mx = np.einsum("knx,ix->kni", Bx.reshape(-1, nn, lx), Qx)
    Fb, eb = fourier(nb)
    s = ein("kni,nbri->rbk", f32(Mx), aW)
    s = ein("eb,rbk->rek", f32(Fb), s)
    den = 1.0 / (c_own[:, None, None] + f32(nu)[None, :, None] + f32(ex)[None, None, :])
    gll = ein("rjk,j->rk", den, f32(qLz * qLz)); glf = ein("rjk,j->rk", den, f32(qLz * qFz))
    s = s / (1 + 2 * gll[:, None] - 2 * glf[:, None] * f32(1 - eb / 2)[None, :, None])
    s = ein("eb,rek->rbk", f32(Fb), s)
    yW = ein("kni,rbk->nbri", f32(Mx), s)
    Z = ein("rji,nbri->nbrj", D, f32(qLx) * yW - f32(qFx) * ea(yW))
    yV = t - SVinv(f32(qLz) * Z - f32(qFz) * dn(Z))
    back = jnp.concatenate([yW, dn(yW), yV, we(yV)], axis=-1).reshape(ND, R, -1)
    got = lax.all_to_all(back, ("narrow", "wide"), split_axis=0, concat_axis=0, tiled=True)
    got = got.transpose(1, 0, 2).reshape(M, -1)
    yb, ya, vb, va = jnp.split(got, [lx, 2 * lx, 2 * lx + lz], axis=-1)
    rh = fh - f32(qLz)[:, None, None] * yb + f32(qFz)[:, None, None] * ya
    rh = rh - vb.T[:, :, None] * f32(qLx) + va.T[:, :, None] * f32(qFx)
    ph = -rh / lam
    p = ein("jz,ix,jmi->mzx", f32(Qz), f32(Qx), ph)
    return p, ein("mi,ix->mx", yb, f32(Qx)), ein("mi,ix->mx", ya, f32(Qx)), ein("mj,jz->mz", vb, f32(Qz)), ein("mj,jz->mz", va, f32(Qz))

def correct(star, press, east, west, north, south, inv_spacing):
    wide_x = jnp.concatenate([west, press, east], axis=2)
    wide_z = jnp.concatenate([south, press, north], axis=1)
    grad_x = (wide_x[:, :, 2:] - wide_x[:, :, :-2]) * 0.5
    grad_y = wall_terms(press, inv_spacing)[0]
    grad_z = (wide_z[:, 2:] - wide_z[:, :-2]) * 0.5
    return star - time_step * jnp.stack([grad_x, grad_y, grad_z])


def periodic_rim(field):
    return extended_2(field, (("narrow", 3), ("wide", 2)), 1)


def shards(velocity, inv_spacing, eigen_wall, to_modes, from_modes):
    star = predict(periodic_rim(velocity), inv_spacing)
    source = diverge(periodic_rim(star), inv_spacing)
    c_all = lax.all_gather(eigen_wall, ("narrow", "wide"), tiled=True)
    nn, nb = lax.axis_size("narrow"), lax.axis_size("wide")
    me = lax.axis_index("narrow") * nb + lax.axis_index("wide")
    c_own = lax.dynamic_index_in_dim(c_all.reshape(-1, nn * nb), me, axis=1, keepdims=False)
    modal = ein("my,yzx->mzx", to_modes, source)
    p, yb, ya, vb, va = solve(modal, c_all, c_own, nb, nn)
    whole = jnp.concatenate([p, (p[:, -1] + yb)[:, None], (p[:, 0] - ya)[:, None]], axis=1)
    whole = ein("ym,mzx->yzx", from_modes, whole)
    side = ein("ym,mse->yse", from_modes, jnp.stack([p[:, :, -1] + vb, p[:, :, 0] - va], axis=2))
    press = whole[:, :-2]
    return correct(star, press, side[:, :, :1], side[:, :, 1:], whole[:, -2:-1], whole[:, -1:], inv_spacing)


def solution(mesh):
    in_specs = (P(None, None, "wide", "narrow"), P(), P(("narrow", "wide")), P(), P())
    out_specs = P(None, None, "wide", "narrow")
    return jax.shard_map(shards, mesh=mesh, in_specs=in_specs, out_specs=out_specs, check_vma=False)
```

```python
import functools
import math

import jax
import numpy as np
import jax.numpy as jnp
from jax import lax
from jax.experimental import pallas as pl
from jax.experimental.pallas import tpu as pltpu
from jax.sharding import PartitionSpec as P

NX = 512
NZ = 512


time_step = 0.1
viscosity = 0.5


MESH = pl.DeviceIdType.MESH
LZ = 16
LX = 128
NY = 384
ROWS = NY * LZ
GROUPS = NY // LX


def first_kernel(nn, nb, v_hbm, spacing, eig, star_hbm, source, walls,
                 v, star, src, zsend, zrecv, xsend, xrecv, s2send, s2recv, x0send, x0recv,
                 load_sem, store_sem, z_ss, z_rs, x_ss, x_rs, s2_ss, s2_rs, x0_ss, x0_rs, e_ss, e_rs):
    me_n = lax.axis_index("narrow")
    me_b = lax.axis_index("wide")
    ring = nb // 4
    layer = me_b // ring
    spot = lax.rem(me_b, ring)
    up = (me_n, lax.rem(me_b + 1, nb))
    down = (me_n, lax.rem(me_b + nb - 1, nb))
    right = (lax.rem(me_n + 1, nn), me_b)
    left = (lax.rem(me_n + nn - 1, nn), me_b)

    loads = [pltpu.make_async_copy(v_hbm.at[c], v.at[c, pl.ds(LZ, ROWS)], load_sem.at[c]) for c in range(3)]
    for c in (2, 0, 1):
        loads[c].start()

    barrier = pltpu.get_barrier_semaphore()
    narrow_peers = [(lax.rem(me_n + k, nn), me_b) for k in range(1, nn)]
    spot_peers = [(me_n, layer * ring + lax.rem(spot + k, ring)) for k in range(1, ring)]
    layer_peers = [(me_n, lax.rem(layer + k, 4) * ring + spot) for k in range(1, 4)]
    greeted = [up, down] + narrow_peers + spot_peers + layer_peers
    for peer in greeted:
        pl.semaphore_signal(barrier, inc=1, device_id=peer, device_id_type=MESH)

    zero = jnp.zeros((LZ, LX), jnp.float32)
    for c in range(3):
        v[c, pl.ds(0, LZ), :] = zero
        v[c, pl.ds(LZ + ROWS, LZ), :] = zero
        star[c, pl.ds(0, LZ), :] = zero
        star[c, pl.ds(LZ + ROWS, LZ), :] = zero
    lane1 = lax.broadcasted_iota(jnp.int32, (1, LX), 1)
    row = jnp.where(lane1 == 0, eig[0], jnp.where(lane1 == 1, eig[1], jnp.where(lane1 == 2, eig[2], 0.0)))
    my_wall = me_b * nn + me_n
    walls[my_wall] = row
    pl.semaphore_wait(barrier, len(greeted))

    def share(peers, at, count, stage):
        for k, peer in enumerate(peers):
            pltpu.make_async_remote_copy(
                src_ref=walls.at[pl.ds(at, count)], dst_ref=walls.at[pl.ds(at, count)],
                send_sem=e_ss.at[stage], recv_sem=e_rs.at[stage], device_id=peer, device_id_type=MESH).start()

    def share_wait(peers, count, stage):
        n = len(peers) * count
        w = pltpu.make_async_remote_copy(
            src_ref=walls.at[pl.ds(0, n)], dst_ref=walls.at[pl.ds(0, n)],
            send_sem=e_ss.at[stage], recv_sem=e_rs.at[stage], device_id=peers[0], device_id_type=MESH)
        w.wait_send()
        w.wait_recv()

    def remote(src_ref, dst_ref, ss, rs, peer):
        return pltpu.make_async_remote_copy(src_ref=src_ref, dst_ref=dst_ref, send_sem=ss, recv_sem=rs,
                                            device_id=peer, device_id_type=MESH)

    lane = lax.broadcasted_iota(jnp.int32, (LZ, LX), 1)
    level = lax.broadcasted_iota(jnp.int32, (LZ, LX), 0)

    def pack(ref, c, g):
        def step(yy, carry):
            last, first = carry
            plane = ref[c, pl.ds(pl.multiple_of(LZ + (g * LX + yy) * LZ, LZ), LZ), :]
            turned = pltpu.roll(plane, lax.rem(yy + 1, LX), 1)
            last = jnp.where(lane == yy, turned, last)
            first = jnp.where(lane == lax.rem(yy + 1, LX), turned, first)
            return last, first
        last, first = lax.fori_loop(0, LX, step, (zero, zero), unroll=8)
        return last, pltpu.roll(first, LX - 1, 1)

    share(narrow_peers, my_wall, 1, 0)
    zcopies, xcopies = [], []
    for c in (2, 0, 1):
        loads[c].wait()
        zsend[0, c] = v[c, pl.ds(LZ + LZ - 1, NY, stride=LZ), :]
        zsend[1, c] = v[c, pl.ds(LZ, NY, stride=LZ), :]
        for side, peer in ((0, up), (1, down)):
            cp = remote(zsend.at[side, c], zrecv.at[side, c], z_ss.at[side, c], z_rs.at[side, c], peer)
            cp.start()
            zcopies.append(cp)
        for g in range(GROUPS):
            last, first = pack(v, c, g)
            xsend[0, c, g] = last
            xsend[1, c, g] = first
        for side, peer in ((0, right), (1, left)):
            cp = remote(xsend.at[side, c], xrecv.at[side, c], x_ss.at[side, c], x_rs.at[side, c], peer)
            cp.start()
            xcopies.append(cp)

    share_wait(narrow_peers, 1, 0)
    share(spot_peers, me_b * nn, nn, 1)
    for cp in xcopies:
        cp.wait_recv()

    def predict_plane(y, _):
        g = y // LX
        yy = lax.rem(y, LX)
        base = pl.multiple_of(LZ + y * LZ, LZ)
        s = spacing[y]
        centre = [v[c, pl.ds(base, LZ), :] for c in range(3)]
        a_e = 0.05 - 0.05 * centre[0]
        a_w = 0.05 + 0.05 * centre[0]
        a_n = jnp.where(level == LZ - 1, 0.0, 0.05 - 0.05 * centre[2])
        a_s = jnp.where(level == 0, 0.0, 0.05 + 0.05 * centre[2])
        curve = 0.05 * s * s
        slope = (0.05 * s) * centre[1]
        a_u = curve - slope
        a_l = curve + slope
        a_c = 0.8 - 2.0 * curve
        to_last = lax.rem(2 * LX - 1 - yy, LX)
        to_first = lax.rem(LX - yy, LX)
        for c in range(3):
            f = centre[c]
            upper = v[c, pl.ds(base + LZ, LZ), :]
            lower = v[c, pl.ds(base - LZ, LZ), :]
            north = pltpu.roll(f, LZ - 1, 0)
            south = pltpu.roll(f, 1, 0)
            east = jnp.where(lane == LX - 1, pltpu.roll(xrecv[1, c, g], to_last, 1), pltpu.roll(f, LX - 1, 1))
            west = jnp.where(lane == 0, pltpu.roll(xrecv[0, c, g], to_first, 1), pltpu.roll(f, 1, 1))
            star[c, pl.ds(base, LZ), :] = (
                a_c * f + a_e * east + a_w * west + (a_n * north + a_s * south) + (a_u * upper + a_l * lower))
        return 0

    lax.fori_loop(0, NY, predict_plane, 0, unroll=2)

    share_wait(spot_peers, nn, 1)
    share(layer_peers, layer * ring * nn, ring * nn, 2)
    for cp in zcopies:
        cp.wait_recv()
    part = 96
    for c in (2, 0, 1):
        for k in range(NY // part):
            hi = LZ + k * part * LZ + LZ - 1
            lo = LZ + k * part * LZ
            rows = pl.ds(k * part, part)
            top = star[c, pl.ds(hi, part, stride=LZ), :] + zrecv[1, c, rows, :] * (
                0.05 - 0.05 * v[2, pl.ds(hi, part, stride=LZ), :])
            low = star[c, pl.ds(lo, part, stride=LZ), :] + zrecv[0, c, rows, :] * (
                0.05 + 0.05 * v[2, pl.ds(lo, part, stride=LZ), :])
            star[c, pl.ds(hi, part, stride=LZ), :] = top
            star[c, pl.ds(lo, part, stride=LZ), :] = low
            if c == 2:
                s2send[0, rows, :] = top
                s2send[1, rows, :] = low
        if c == 2:
            s2copies = [remote(s2send.at[side], s2recv.at[side], s2_ss.at[side], s2_rs.at[side], peer)
                        for side, peer in ((0, up), (1, down))]
            for cp in s2copies:
                cp.start()
        if c == 0:
            for g in range(GROUPS):
                last, first = pack(star, 0, g)
                x0send[0, g] = last
                x0send[1, g] = first
            x0copies = [remote(x0send.at[side], x0recv.at[side], x0_ss.at[side], x0_rs.at[side], peer)
                        for side, peer in ((0, right), (1, left))]
            for cp in x0copies:
                cp.start()
    stores = [pltpu.make_async_copy(star.at[c, pl.ds(LZ, ROWS)], star_hbm.at[c], store_sem.at[c]) for c in range(3)]
    for cp in stores:
        cp.start()
    for cp in x0copies:
        cp.wait_recv()

    def diverge_plane(y, _):
        g = y // LX
        yy = lax.rem(y, LX)
        base = pl.multiple_of(LZ + y * LZ, LZ)
        s = 5.0 * spacing[y]
        to_last = lax.rem(2 * LX - 1 - yy, LX)
        to_first = lax.rem(LX - yy, LX)
        f = star[0, pl.ds(base, LZ), :]
        east = jnp.where(lane == LX - 1, pltpu.roll(x0recv[1, g], to_last, 1), pltpu.roll(f, LX - 1, 1))
        west = jnp.where(lane == 0, pltpu.roll(x0recv[0, g], to_first, 1), pltpu.roll(f, 1, 1))
        h = star[2, pl.ds(base, LZ), :]
        north = jnp.where(level == LZ - 1, 0.0, pltpu.roll(h, LZ - 1, 0))
        south = jnp.where(level == 0, 0.0, pltpu.roll(h, 1, 0))
        rise = star[1, pl.ds(base + LZ, LZ), :] - star[1, pl.ds(base - LZ, LZ), :]
        src[pl.ds(pl.multiple_of(y * LZ, LZ), LZ), :] = 5.0 * ((east - west) + (north - south)) + s * rise
        return 0

    lax.fori_loop(0, NY, diverge_plane, 0, unroll=4)
    for z in range(1, LZ - 1):
        source[z] = src[pl.ds(z, NY, stride=LZ), :]
    for cp in s2copies:
        cp.wait_recv()
    source[0] = src[pl.ds(0, NY, stride=LZ), :] - 5.0 * s2recv[0]
    source[LZ - 1] = src[pl.ds(LZ - 1, NY, stride=LZ), :] + 5.0 * s2recv[1]
    share_wait(layer_peers, ring * nn, 2)
    for cp in zcopies + xcopies + s2copies + x0copies:
        cp.wait_send()
    for cp in stores:
        cp.wait()


def first_part(velocity, inv_spacing, eigen_wall):
    nn, nb = lax.axis_size("narrow"), lax.axis_size("wide")
    f32 = jnp.float32
    any_, vmem, smem = (pl.BlockSpec(memory_space=m) for m in (pl.ANY, pltpu.VMEM, pltpu.SMEM))
    dma = pltpu.SemaphoreType.DMA
    return pl.pallas_call(
        functools.partial(first_kernel, nn, nb),
        out_shape=(jax.ShapeDtypeStruct((3, ROWS, LX), f32), jax.ShapeDtypeStruct((LZ, NY, LX), f32),
                   jax.ShapeDtypeStruct((nn * nb, 1, LX), f32)),
        in_specs=[any_, smem, smem],
        out_specs=(any_, vmem, vmem),
        scratch_shapes=[
            pltpu.VMEM((3, ROWS + 2 * LZ, LX), f32), pltpu.VMEM((3, ROWS + 2 * LZ, LX), f32), pltpu.VMEM((ROWS, LX), f32),
            pltpu.VMEM((2, 3, NY, LX), f32), pltpu.VMEM((2, 3, NY, LX), f32),
            pltpu.VMEM((2, 3, GROUPS, LZ, LX), f32), pltpu.VMEM((2, 3, GROUPS, LZ, LX), f32),
            pltpu.VMEM((2, NY, LX), f32), pltpu.VMEM((2, NY, LX), f32),
            pltpu.VMEM((2, GROUPS, LZ, LX), f32), pltpu.VMEM((2, GROUPS, LZ, LX), f32),
            dma((3,)), dma((3,)), dma((2, 3)), dma((2, 3)), dma((2, 3)), dma((2, 3)),
            dma((2,)), dma((2,)), dma((2,)), dma((2,)), dma((3,)), dma((3,)),
        ],
        compiler_params=pltpu.CompilerParams(collective_id=0, has_side_effects=True, vmem_limit_bytes=56 * 1024 * 1024),
        name="predict_diverge",
    )(velocity.reshape(3, ROWS, LX), inv_spacing, eigen_wall)


def wall_terms(field, inv_spacing):
    zero = jnp.zeros_like(field[..., :1, :, :])
    upper = jnp.concatenate([field[..., 1:, :, :], zero], axis=-3)
    lower = jnp.concatenate([zero, field[..., :-1, :, :]], axis=-3)
    scale = inv_spacing[:, None, None]
    return ((upper - lower) * 0.5 * scale, (upper - 2.0 * field + lower) * scale * scale)


def cosines(n):
    j = np.arange(n)[:, None]; z = np.arange(n)[None, :]
    q = np.cos(np.pi * j * (z + 0.5) / n) * np.where(j == 0, math.sqrt(1 / n), math.sqrt(2 / n))
    return q, 2 - 2 * np.cos(np.pi * np.arange(n) / n)

def fourier(n):
    r = np.arange(n)[:, None]; c = np.arange(n)[None, :]
    mid = n // 2
    k = np.where(r <= mid, r, r - mid)
    ph = (k * c % n) * (2 * np.pi / n)
    w = np.where(r <= mid, np.cos(ph), np.sin(ph))
    s = np.where((r == 0) | (r == mid), math.sqrt(1 / n), math.sqrt(2 / n))
    return w * s, 2 - 2 * np.cos(2 * np.pi * k[:, 0] / n)

prec = lax.Precision.HIGH
ein = functools.partial(jnp.einsum, precision=prec)
f32 = lambda a: jnp.asarray(np.asarray(a, np.float32))

def solve(modal, c_all, c_own, nb, nn):
    M, lz, lx = modal.shape
    ND = nb * nn
    R = M // ND
    Qz, nu = cosines(lz); Qx, mu = cosines(lx)
    qLz, qFz = Qz[:, -1], Qz[:, 0]; qLx, qFx = Qx[:, -1], Qx[:, 0]
    lam = c_all[None, :, None] + f32(nu)[:, None, None] + f32(mu)[None, None, :]
    fh = ein("jz,ix,mzx->jmi", f32(Qz), f32(Qx), modal)
    gh = fh / lam
    zl = ein("j,jmi->mi", f32(qLz), gh); zf = ein("j,jmi->mi", f32(qFz), gh)
    xl = ein("i,jmi->mj", f32(qLx), gh); xf = ein("i,jmi->mj", f32(qFx), gh)
    send = jnp.concatenate([zl, zf, xl, xf], axis=1).reshape(R, ND, -1).transpose(1, 0, 2)
    recv = lax.all_to_all(send, ("narrow", "wide"), split_axis=0, concat_axis=0, tiled=True)
    recv = recv.reshape(nn, nb, R, -1)
    zl, zf, xl, xf = jnp.split(recv, [lx, 2 * lx, 2 * lx + lz], axis=-1)
    up = lambda a: jnp.roll(a, -1, axis=1)
    dn = lambda a: jnp.roll(a, 1, axis=1)
    ea = lambda a: jnp.roll(a, -1, axis=0)
    we = lambda a: jnp.roll(a, 1, axis=0)
    aW = zl - up(zf)
    aV = xl - ea(xf)
    D = 1.0 / (c_own[:, None, None] + f32(nu)[None, :, None] + f32(mu)[None, None, :])
    hll = ein("rji,i->rj", D, f32(qLx * qLx)); hlf = ein("rji,i->rj", D, f32(qLx * qFx))
    Fn, en = fourier(nn)
    lamn = 1 + 2 * hll[..., None] - 2 * hlf[..., None] * f32(1 - en / 2)
    def SVinv(a):
        t = ein("en,nbrj->ebrj", f32(Fn), a)
        t = t / lamn.transpose(2, 0, 1)[:, None]
        return ein("en,ebrj->nbrj", f32(Fn), t)
    t = SVinv(aV)
    T = f32(qLz) * t - f32(qFz) * up(t)
    TD = ein("nbrj,rji->nbri", T, D)
    aW = aW - (f32(qLx) * TD - f32(qFx) * we(TD))
    Bx, ex = fourier(nn * lx)
    Mx = np.einsum("knx,ix->kni", Bx.reshape(-1, nn, lx), Qx)
    Fb, eb = fourier(nb)
    s = ein("kni,nbri->rbk", f32(Mx), aW)
    s = ein("eb,rbk->rek", f32(Fb), s)
    den = 1.0 / (c_own[:, None, None] + f32(nu)[None, :, None] + f32(ex)[None, None, :])
    gll = ein("rjk,j->rk", den, f32(qLz * qLz)); glf = ein("rjk,j->rk", den, f32(qLz * qFz))
    s = s / (1 + 2 * gll[:, None] - 2 * glf[:, None] * f32(1 - eb / 2)[None, :, None])
    s = ein("eb,rek->rbk", f32(Fb), s)
    yW = ein("kni,rbk->nbri", f32(Mx), s)
    Z = ein("rji,nbri->nbrj", D, f32(qLx) * yW - f32(qFx) * ea(yW))
    yV = t - SVinv(f32(qLz) * Z - f32(qFz) * dn(Z))
    back = jnp.concatenate([yW, dn(yW), yV, we(yV)], axis=-1).reshape(ND, R, -1)
    got = lax.all_to_all(back, ("narrow", "wide"), split_axis=0, concat_axis=0, tiled=True)
    got = got.transpose(1, 0, 2).reshape(M, -1)
    yb, ya, vb, va = jnp.split(got, [lx, 2 * lx, 2 * lx + lz], axis=-1)
    rh = fh - f32(qLz)[:, None, None] * yb + f32(qFz)[:, None, None] * ya
    rh = rh - vb.T[:, :, None] * f32(qLx) + va.T[:, :, None] * f32(qFx)
    ph = -rh / lam
    p = ein("jz,ix,jmi->mzx", f32(Qz), f32(Qx), ph)
    return p, ein("mi,ix->mx", yb, f32(Qx)), ein("mi,ix->mx", ya, f32(Qx)), ein("mj,jz->mz", vb, f32(Qz)), ein("mj,jz->mz", va, f32(Qz))

def correct(star, press, east, west, north, south, inv_spacing):
    wide_x = jnp.concatenate([west, press, east], axis=2)
    wide_z = jnp.concatenate([south, press, north], axis=1)
    grad_x = (wide_x[:, :, 2:] - wide_x[:, :, :-2]) * 0.5
    grad_y = wall_terms(press, inv_spacing)[0]
    grad_z = (wide_z[:, 2:] - wide_z[:, :-2]) * 0.5
    return star - time_step * jnp.stack([grad_x, grad_y, grad_z])


def shards(velocity, inv_spacing, eigen_wall, to_modes, from_modes):
    star, source, walls = first_part(velocity, inv_spacing, eigen_wall)
    star = star.reshape(3, NY, LZ, LX)
    nn, nb = lax.axis_size("narrow"), lax.axis_size("wide")
    c_all = walls[:, 0, :3].reshape(nb, nn, 3).transpose(1, 0, 2).reshape(-1)
    me = lax.axis_index("narrow") * nb + lax.axis_index("wide")
    c_own = lax.dynamic_index_in_dim(c_all.reshape(-1, nn * nb), me, axis=1, keepdims=False)
    modal = ein("my,zyx->mzx", to_modes, source)
    p, yb, ya, vb, va = solve(modal, c_all, c_own, nb, nn)
    whole = jnp.concatenate([p, (p[:, -1] + yb)[:, None], (p[:, 0] - ya)[:, None]], axis=1)
    whole = ein("ym,mzx->yzx", from_modes, whole)
    side = ein("ym,mse->yse", from_modes, jnp.stack([p[:, :, -1] + vb, p[:, :, 0] - va], axis=2))
    press = whole[:, :-2]
    return correct(star, press, side[:, :, :1], side[:, :, 1:], whole[:, -2:-1], whole[:, -1:], inv_spacing)


def solution(mesh):
    in_specs = (P(None, None, "wide", "narrow"), P(), P(("narrow", "wide")), P(), P())
    out_specs = P(None, None, "wide", "narrow")
    return jax.shard_map(shards, mesh=mesh, in_specs=in_specs, out_specs=out_specs, check_vma=False)
```

```python
import functools
import math

import jax
import jax.numpy as jnp
import ml_dtypes
import numpy as np
from jax import lax
from jax.experimental import pallas as pl
from jax.experimental.pallas import tpu as pltpu
from jax.sharding import PartitionSpec as P

MESH = pl.DeviceIdType.MESH
LZ = 16
LX = 128
NY = 384
ROWS = NY * LZ
GROUPS = NY // LX


def first_kernel(nn, nb, v_hbm, spacing, eig, star_hbm, source, walls,
                 v, star, src, zsend, zrecv, xsend, xrecv, s2send, s2recv, x0send, x0recv,
                 load_sem, store_sem, z_ss, z_rs, x_ss, x_rs, s2_ss, s2_rs, x0_ss, x0_rs, e_ss, e_rs):
    me_n = lax.axis_index("narrow")
    me_b = lax.axis_index("wide")
    ring = nb // 4
    layer = me_b // ring
    spot = lax.rem(me_b, ring)
    up = (me_n, lax.rem(me_b + 1, nb))
    down = (me_n, lax.rem(me_b + nb - 1, nb))
    right = (lax.rem(me_n + 1, nn), me_b)
    left = (lax.rem(me_n + nn - 1, nn), me_b)

    loads = [pltpu.make_async_copy(v_hbm.at[c], v.at[c, pl.ds(LZ, ROWS)], load_sem.at[c]) for c in range(3)]
    for c in (2, 0, 1):
        loads[c].start()

    barrier = pltpu.get_barrier_semaphore()
    narrow_peers = [(lax.rem(me_n + k, nn), me_b) for k in range(1, nn)]
    spot_peers = [(me_n, layer * ring + lax.rem(spot + k, ring)) for k in range(1, ring)]
    layer_peers = [(me_n, lax.rem(layer + k, 4) * ring + spot) for k in range(1, 4)]
    greeted = [up, down] + narrow_peers + spot_peers + layer_peers
    for peer in greeted:
        pl.semaphore_signal(barrier, inc=1, device_id=peer, device_id_type=MESH)

    zero = jnp.zeros((LZ, LX), jnp.float32)
    for c in range(3):
        v[c, pl.ds(0, LZ), :] = zero
        v[c, pl.ds(LZ + ROWS, LZ), :] = zero
        star[c, pl.ds(0, LZ), :] = zero
        star[c, pl.ds(LZ + ROWS, LZ), :] = zero
    lane1 = lax.broadcasted_iota(jnp.int32, (1, LX), 1)
    row = jnp.where(lane1 == 0, eig[0], jnp.where(lane1 == 1, eig[1], jnp.where(lane1 == 2, eig[2], 0.0)))
    my_wall = me_b * nn + me_n
    walls[my_wall] = row
    pl.semaphore_wait(barrier, len(greeted))

    def share(peers, at, count, stage):
        for k, peer in enumerate(peers):
            pltpu.make_async_remote_copy(
                src_ref=walls.at[pl.ds(at, count)], dst_ref=walls.at[pl.ds(at, count)],
                send_sem=e_ss.at[stage], recv_sem=e_rs.at[stage], device_id=peer, device_id_type=MESH).start()

    def share_wait(peers, count, stage):
        n = len(peers) * count
        w = pltpu.make_async_remote_copy(
            src_ref=walls.at[pl.ds(0, n)], dst_ref=walls.at[pl.ds(0, n)],
            send_sem=e_ss.at[stage], recv_sem=e_rs.at[stage], device_id=peers[0], device_id_type=MESH)
        w.wait_send()
        w.wait_recv()

    def remote(src_ref, dst_ref, ss, rs, peer):
        return pltpu.make_async_remote_copy(src_ref=src_ref, dst_ref=dst_ref, send_sem=ss, recv_sem=rs,
                                            device_id=peer, device_id_type=MESH)

    lane = lax.broadcasted_iota(jnp.int32, (LZ, LX), 1)
    level = lax.broadcasted_iota(jnp.int32, (LZ, LX), 0)

    def pack(ref, c, g):
        def step(yy, carry):
            last, first = carry
            plane = ref[c, pl.ds(pl.multiple_of(LZ + (g * LX + yy) * LZ, LZ), LZ), :]
            turned = pltpu.roll(plane, lax.rem(yy + 1, LX), 1)
            last = jnp.where(lane == yy, turned, last)
            first = jnp.where(lane == lax.rem(yy + 1, LX), turned, first)
            return last, first
        last, first = lax.fori_loop(0, LX, step, (zero, zero), unroll=8)
        return last, pltpu.roll(first, LX - 1, 1)

    share(narrow_peers, my_wall, 1, 0)
    zcopies, xcopies = [], []
    for c in (2, 0, 1):
        loads[c].wait()
        zsend[0, c] = v[c, pl.ds(LZ + LZ - 1, NY, stride=LZ), :]
        zsend[1, c] = v[c, pl.ds(LZ, NY, stride=LZ), :]
        for side, peer in ((0, up), (1, down)):
            cp = remote(zsend.at[side, c], zrecv.at[side, c], z_ss.at[side, c], z_rs.at[side, c], peer)
            cp.start()
            zcopies.append(cp)
        for g in range(GROUPS):
            last, first = pack(v, c, g)
            xsend[0, c, g] = last
            xsend[1, c, g] = first
        for side, peer in ((0, right), (1, left)):
            cp = remote(xsend.at[side, c], xrecv.at[side, c], x_ss.at[side, c], x_rs.at[side, c], peer)
            cp.start()
            xcopies.append(cp)

    share_wait(narrow_peers, 1, 0)
    share(spot_peers, me_b * nn, nn, 1)
    for cp in xcopies:
        cp.wait_recv()

    def predict_plane(y, _):
        g = y // LX
        yy = lax.rem(y, LX)
        base = pl.multiple_of(LZ + y * LZ, LZ)
        s = spacing[y]
        centre = [v[c, pl.ds(base, LZ), :] for c in range(3)]
        a_e = 0.05 - 0.05 * centre[0]
        a_w = 0.05 + 0.05 * centre[0]
        a_n = jnp.where(level == LZ - 1, 0.0, 0.05 - 0.05 * centre[2])
        a_s = jnp.where(level == 0, 0.0, 0.05 + 0.05 * centre[2])
        curve = 0.05 * s * s
        slope = (0.05 * s) * centre[1]
        a_u = curve - slope
        a_l = curve + slope
        a_c = 0.8 - 2.0 * curve
        to_last = lax.rem(2 * LX - 1 - yy, LX)
        to_first = lax.rem(LX - yy, LX)
        for c in range(3):
            f = centre[c]
            upper = v[c, pl.ds(base + LZ, LZ), :]
            lower = v[c, pl.ds(base - LZ, LZ), :]
            north = pltpu.roll(f, LZ - 1, 0)
            south = pltpu.roll(f, 1, 0)
            east = jnp.where(lane == LX - 1, pltpu.roll(xrecv[1, c, g], to_last, 1), pltpu.roll(f, LX - 1, 1))
            west = jnp.where(lane == 0, pltpu.roll(xrecv[0, c, g], to_first, 1), pltpu.roll(f, 1, 1))
            star[c, pl.ds(base, LZ), :] = (
                a_c * f + a_e * east + a_w * west + (a_n * north + a_s * south) + (a_u * upper + a_l * lower))
        return 0

    lax.fori_loop(0, NY, predict_plane, 0, unroll=2)

    share_wait(spot_peers, nn, 1)
    share(layer_peers, layer * ring * nn, ring * nn, 2)
    for cp in zcopies:
        cp.wait_recv()
    part = 96
    for c in (2, 0, 1):
        for k in range(NY // part):
            hi = LZ + k * part * LZ + LZ - 1
            lo = LZ + k * part * LZ
            rows = pl.ds(k * part, part)
            top = star[c, pl.ds(hi, part, stride=LZ), :] + zrecv[1, c, rows, :] * (
                0.05 - 0.05 * v[2, pl.ds(hi, part, stride=LZ), :])
            low = star[c, pl.ds(lo, part, stride=LZ), :] + zrecv[0, c, rows, :] * (
                0.05 + 0.05 * v[2, pl.ds(lo, part, stride=LZ), :])
            star[c, pl.ds(hi, part, stride=LZ), :] = top
            star[c, pl.ds(lo, part, stride=LZ), :] = low
            if c == 2:
                s2send[0, rows, :] = top
                s2send[1, rows, :] = low
        if c == 2:
            s2copies = [remote(s2send.at[side], s2recv.at[side], s2_ss.at[side], s2_rs.at[side], peer)
                        for side, peer in ((0, up), (1, down))]
            for cp in s2copies:
                cp.start()
        if c == 0:
            for g in range(GROUPS):
                last, first = pack(star, 0, g)
                x0send[0, g] = last
                x0send[1, g] = first
            x0copies = [remote(x0send.at[side], x0recv.at[side], x0_ss.at[side], x0_rs.at[side], peer)
                        for side, peer in ((0, right), (1, left))]
            for cp in x0copies:
                cp.start()
    stores = [pltpu.make_async_copy(star.at[c, pl.ds(LZ, ROWS)], star_hbm.at[c], store_sem.at[c]) for c in range(3)]
    for cp in stores:
        cp.start()
    for cp in x0copies:
        cp.wait_recv()

    def diverge_plane(y, _):
        g = y // LX
        yy = lax.rem(y, LX)
        base = pl.multiple_of(LZ + y * LZ, LZ)
        s = 5.0 * spacing[y]
        to_last = lax.rem(2 * LX - 1 - yy, LX)
        to_first = lax.rem(LX - yy, LX)
        f = star[0, pl.ds(base, LZ), :]
        east = jnp.where(lane == LX - 1, pltpu.roll(x0recv[1, g], to_last, 1), pltpu.roll(f, LX - 1, 1))
        west = jnp.where(lane == 0, pltpu.roll(x0recv[0, g], to_first, 1), pltpu.roll(f, 1, 1))
        h = star[2, pl.ds(base, LZ), :]
        north = jnp.where(level == LZ - 1, 0.0, pltpu.roll(h, LZ - 1, 0))
        south = jnp.where(level == 0, 0.0, pltpu.roll(h, 1, 0))
        rise = star[1, pl.ds(base + LZ, LZ), :] - star[1, pl.ds(base - LZ, LZ), :]
        src[pl.ds(pl.multiple_of(y * LZ, LZ), LZ), :] = 5.0 * ((east - west) + (north - south)) + s * rise
        return 0

    lax.fori_loop(0, NY, diverge_plane, 0, unroll=4)
    for z in range(1, LZ - 1):
        source[z] = src[pl.ds(z, NY, stride=LZ), :]
    for cp in s2copies:
        cp.wait_recv()
    source[0] = src[pl.ds(0, NY, stride=LZ), :] - 5.0 * s2recv[0]
    source[LZ - 1] = src[pl.ds(LZ - 1, NY, stride=LZ), :] + 5.0 * s2recv[1]
    share_wait(layer_peers, ring * nn, 2)
    for cp in zcopies + xcopies + s2copies + x0copies:
        cp.wait_send()
    for cp in stores:
        cp.wait()


def first_part(velocity, inv_spacing, eigen_wall):
    nn, nb = lax.axis_size("narrow"), lax.axis_size("wide")
    f32 = jnp.float32
    any_, vmem, smem = (pl.BlockSpec(memory_space=m) for m in (pl.ANY, pltpu.VMEM, pltpu.SMEM))
    dma = pltpu.SemaphoreType.DMA
    return pl.pallas_call(
        functools.partial(first_kernel, nn, nb),
        out_shape=(jax.ShapeDtypeStruct((3, ROWS, LX), f32), jax.ShapeDtypeStruct((LZ, NY, LX), f32),
                   jax.ShapeDtypeStruct((nn * nb, 1, LX), f32)),
        in_specs=[any_, smem, smem],
        out_specs=(any_, vmem, vmem),
        scratch_shapes=[
            pltpu.VMEM((3, ROWS + 2 * LZ, LX), f32), pltpu.VMEM((3, ROWS + 2 * LZ, LX), f32), pltpu.VMEM((ROWS, LX), f32),
            pltpu.VMEM((2, 3, NY, LX), f32), pltpu.VMEM((2, 3, NY, LX), f32),
            pltpu.VMEM((2, 3, GROUPS, LZ, LX), f32), pltpu.VMEM((2, 3, GROUPS, LZ, LX), f32),
            pltpu.VMEM((2, NY, LX), f32), pltpu.VMEM((2, NY, LX), f32),
            pltpu.VMEM((2, GROUPS, LZ, LX), f32), pltpu.VMEM((2, GROUPS, LZ, LX), f32),
            dma((3,)), dma((3,)), dma((2, 3)), dma((2, 3)), dma((2, 3)), dma((2, 3)),
            dma((2,)), dma((2,)), dma((2,)), dma((2,)), dma((3,)), dma((3,)),
        ],
        compiler_params=pltpu.CompilerParams(collective_id=0, has_side_effects=True, vmem_limit_bytes=56 * 1024 * 1024),
        name="predict_diverge",
    )(velocity.reshape(3, ROWS, LX), inv_spacing, eigen_wall)


def split(a):
    high = a.astype(jnp.bfloat16)
    return high, (a - high.astype(jnp.float32)).astype(jnp.bfloat16)


def mm(a, b):
    return jnp.dot(a, b, preferred_element_type=jnp.float32)


def mm3(a, b_high, b_low):
    high, low = split(a)
    return mm(high, b_high) + mm(low, b_high) + mm(high, b_low)


def cosines(n):
    j = np.arange(n)[:, None]
    z = np.arange(n)[None, :]
    q = np.cos(np.pi * j * (z + 0.5) / n) * np.where(j == 0, math.sqrt(1 / n), math.sqrt(2 / n))
    return q, 2 - 2 * np.cos(np.pi * np.arange(n) / n)


def fourier(n):
    r = np.arange(n)[:, None]
    c = np.arange(n)[None, :]
    mid = n // 2
    k = np.where(r <= mid, r, r - mid)
    phase = (k * c % n) * (2 * np.pi / n)
    waves = np.where(r <= mid, np.cos(phase), np.sin(phase))
    weight = np.where((r == 0) | (r == mid), math.sqrt(1 / n), math.sqrt(2 / n))
    return waves * weight, 2 - 2 * np.cos(2 * np.pi * k[:, 0] / n)


def halves(a):
    a = np.asarray(a, np.float32)
    high = a.astype(ml_dtypes.bfloat16)
    return high, (a - high.astype(np.float32)).astype(ml_dtypes.bfloat16)


def paired(a):
    high, low = halves(a)
    return np.block([[high, low], [high, np.zeros_like(low)]])


QZ, NU = cosines(LZ)
QX, MU = cosines(LX)
QZL, QZF = QZ[:, -1], QZ[:, 0]
QXL, QXF = QX[:, -1], QX[:, 0]
SLOT = 2 * LZ
R = 3


def to_cosines(x):
    n = len(x)
    out = [None] * n
    e = [x[z] + x[n - 1 - z] for z in range(n // 2)]
    o = [x[z] - x[n - 1 - z] for z in range(n // 2)]
    ee = [e[z] + e[n // 2 - 1 - z] for z in range(n // 4)]
    eo = [e[z] - e[n // 2 - 1 - z] for z in range(n // 4)]
    for j in range(n):
        part = o if j % 2 else (eo if j % 4 else ee)
        out[j] = sum(float(QZ[j, z]) * part[z] for z in range(len(part)))
    return out


def from_cosines(f):
    n = len(f)
    even, out = [None] * (n // 2), [None] * n
    for z in range(n // 4):
        a = sum(float(QZ[j, z]) * f[j] for j in range(0, n, 4))
        b = sum(float(QZ[j, z]) * f[j] for j in range(2, n, 4))
        even[z], even[n // 2 - 1 - z] = a + b, a - b
    for z in range(n // 2):
        odd = sum(float(QZ[j, z]) * f[j] for j in range(1, n, 2))
        out[z], out[n - 1 - z] = even[z] + odd, even[z] - odd
    return out


def solve_kernel(nn, nb, source, to_modes, walls, own, mu_row, xw, edge_hl, edge_h, nu_lane, nu_row, mu_col, q_lane,
                 spec_h, spec_l, back_h, back_l, turn_h, turn_l, unturn_h, unturn_l, cos_b, ex_row,
                 fh, got, gz, gh, zl, zf, send, recv, back, s1, r1, s2, r2, loc):
    f32 = jnp.float32
    nd = nn * nb
    me_n = lax.axis_index("narrow")
    me_b = lax.axis_index("wide")
    me = me_n * nb + me_b
    barrier = pltpu.get_barrier_semaphore()

    def greet(k, _):
        d = lax.rem(me + k, nd)
        pl.semaphore_signal(barrier, inc=1, device_id=(d // nb, lax.rem(d, nb)), device_id_type=MESH)
        return 0

    lax.fori_loop(1, nd, greet, 0)

    t_high, t_low = split(to_modes[...])
    for z in range(0, LZ, 2):
        s_high, s_low = split(jnp.concatenate([source[z], source[z + 1]], axis=1))
        modal = mm(t_high, s_high) + mm(t_low, s_high) + mm(t_high, s_low)
        for k in range(2):
            high, low = split(modal[:, k * LX:(k + 1) * LX])
            both = mm(jnp.concatenate([high, low], axis=1), xw[...])
            gz[z + k] = both[:, :LX] + both[:, LX:]

    def chunk(k, _):
        rows = pl.ds(pl.multiple_of(k * 8, 8), 8)
        f = to_cosines([gz[z, rows, :] for z in range(LZ)])
        base = walls[rows, :] + mu_row[...]
        sums = [None, None]
        for j in range(LZ):
            fh[j, rows, :] = f[j]
            g = f[j] * pl.reciprocal(base + float(NU[j]))
            gh[j, rows, :] = g
            term = float(QZL[j]) * g
            sums[j % 2] = term if sums[j % 2] is None else sums[j % 2] + term
        zl[rows, :] = sums[0] + sums[1]
        zf[rows, :] = sums[0] - sums[1]
        return 0

    lax.fori_loop(0, NY // 8, chunk, 0)
    edge = jnp.zeros((NY, LX), f32)
    for j in range(0, LZ, 2):
        high, low = split(jnp.concatenate([gh[j], gh[j + 1]], axis=1))
        both = mm(high, edge_hl[j // 2])
        edge = edge + both[:, :LX] + both[:, LX:] + mm(low, edge_h[j // 2])
    packed = edge[:nd]
    for r in range(R):
        rows = pl.ds(r * nd, nd)
        send[pl.ds(r, nd, stride=8), :] = zl[rows, :]
        send[pl.ds(R + r, nd, stride=8), :] = zf[rows, :]
        if r:
            packed = packed + pltpu.roll(edge[r * nd:(r + 1) * nd], SLOT * r, 1)
    send[pl.ds(2 * R, nd, stride=8), :] = packed
    send[pl.ds(2 * R + 1, nd, stride=8), :] = jnp.zeros((nd, LX), f32)
    pl.semaphore_wait(barrier, nd - 1)

    def ship(src, dst, ss, rs):
        def go(k, _):
            d = lax.rem(me + k, nd)
            pltpu.make_async_remote_copy(
                src_ref=src.at[pl.ds(pl.multiple_of(d * 8, 8), 8)], dst_ref=dst.at[pl.ds(pl.multiple_of(me * 8, 8), 8)],
                send_sem=ss, recv_sem=rs, device_id=(d // nb, lax.rem(d, nb)), device_id_type=MESH).start()
            return 0
        lax.fori_loop(1, nd, go, 0)
        mine = pl.ds(pl.multiple_of(me * 8, 8), 8)
        dst[mine, :] = src[mine, :]
        most = pl.ds(0, (nd - 1) * 8)
        return pltpu.make_async_remote_copy(src_ref=src.at[most], dst_ref=dst.at[most], send_sem=ss, recv_sem=rs,
                                            device_id=(me_n, me_b), device_id_type=MESH)

    out = ship(send, recv, s1, r1)

    lane = lax.broadcasted_iota(jnp.int32, (1, LX), 1)
    owner_lane = jnp.where(lane < SLOT, own[0], jnp.where(lane < 2 * SLOT, own[1], own[2]))
    rowid = lax.broadcasted_iota(jnp.int32, (LX, LX), 0)
    owner_row = jnp.where(rowid < SLOT, own[0], jnp.where(rowid < 2 * SLOT, own[1], own[2]))
    low_half = lax.rem(lane, SLOT) < LZ
    d_rows = pl.reciprocal(owner_row + nu_row[...] + mu_row[...])
    d_cols = pl.reciprocal(owner_lane + nu_lane[...] + mu_col[...])
    qxl, qxf = q_lane[0:1], q_lane[1:2]
    qzl = jnp.where(low_half, q_lane[2:3], 0.0)
    qzf = jnp.where(low_half, q_lane[3:4], 0.0)
    hll = jnp.sum(d_cols * q_lane[8:8 + LX], axis=0, keepdims=True)
    hlf = jnp.sum(d_cols * q_lane[8 + LX:8 + 2 * LX], axis=0, keepdims=True)
    l0, l1, l2 = (1.0 / (1 + 2 * hll - 2 * hlf), 1.0 / (1 + 2 * hll), 1.0 / (1 + 2 * hll + 2 * hlf))
    k0, k1, k2 = (0.25 * (l0 + 2 * l1 + l2), 0.25 * (l0 - l2), 0.25 * (l0 - 2 * l1 + l2))
    dr_h, dr_l = split(d_rows)
    dc_h, dc_l = split(d_cols)
    scale = []
    for r in range(R):
        gll = jnp.zeros_like(ex_row[...])
        glf = jnp.zeros_like(ex_row[...])
        for j in range(LZ):
            g = 1.0 / (own[r] + float(NU[j]) + ex_row[...])
            gll = gll + float(QZL[j] ** 2) * g
            glf = glf + float(QZL[j] * QZF[j]) * g
        scale.append(1.0 / (1 + 2 * gll - 2 * glf * cos_b[...]))
    scale = jnp.concatenate(scale, axis=0)

    def coupled(a):
        return [k0 * a[n] + k1 * (a[(n + 1) % nn] + a[(n - 1) % nn]) + k2 * a[(n + 2) % nn] for n in range(nn)]

    def ahead(a):
        return pltpu.roll(a, nb - 1, 0)

    def behind(a):
        return pltpu.roll(a, 1, 0)

    def blocks(a):
        return [a[n * nb:(n + 1) * nb] for n in range(nn)]

    out.wait_recv()
    x = blocks(recv[pl.ds(2 * R, nd, stride=8), :])
    t = coupled([jnp.where(low_half, x[n] - pltpu.roll(x[(n + 1) % nn], LX - LZ, 1), 0.0) for n in range(nn)])
    big = jnp.concatenate([qzl * t[n] - qzf * ahead(t[n]) for n in range(nn)], axis=0)
    lines = []
    for r in range(R):
        mine = (lane >= SLOT * r) & (lane < SLOT * (r + 1))
        td = blocks(mm3(jnp.where(mine, big, 0.0), dr_h, dr_l))
        last = blocks(recv[pl.ds(r, nd, stride=8), :])
        first = blocks(recv[pl.ds(R + r, nd, stride=8), :])
        lines.append(jnp.concatenate(
            [last[n] - ahead(first[n]) - (qxl * td[n] - qxf * td[(n - 1) % nn]) for n in range(nn)], axis=1))
    s = mm3(jnp.concatenate(lines, axis=0), spec_h[...], spec_l[...])
    s = jnp.concatenate([s, jnp.zeros((LX - R * nb, nn * LX), f32)], axis=0)
    s_h, s_l = split(s)
    s = mm(turn_h[...], s_h) + mm(turn_l[...], s_h) + mm(turn_h[...], s_l)
    s = jnp.concatenate([s[:R * nb] * scale, s[R * nb:]], axis=0)
    s_h, s_l = split(s)
    s = mm(unturn_h[...], s_h) + mm(unturn_l[...], s_h) + mm(unturn_h[...], s_l)
    y = mm3(s[:R * nb], back_h[...], back_l[...])
    zsum = jnp.zeros((nd, LX), f32)
    for r in range(R):
        yr = [y[r * nb:(r + 1) * nb, n * LX:(n + 1) * LX] for n in range(nn)]
        back[pl.ds(r, nd, stride=8), :] = jnp.concatenate(yr, axis=0)
        back[pl.ds(R + r, nd, stride=8), :] = jnp.concatenate([behind(a) for a in yr], axis=0)
        mine = (lane >= SLOT * r) & (lane < SLOT * (r + 1))
        ends = jnp.concatenate([qxl * yr[n] - qxf * yr[(n + 1) % nn] for n in range(nn)], axis=0)
        zsum = zsum + jnp.where(mine, mm3(ends, dc_h, dc_l), 0.0)
    zs = blocks(zsum)
    u = coupled([qzl * zs[n] - qzf * behind(zs[n]) for n in range(nn)])
    w = [jnp.where(low_half, t[n] - u[n], 0.0) for n in range(nn)]
    back[pl.ds(2 * R, nd, stride=8), :] = jnp.concatenate(
        [w[n] + pltpu.roll(w[(n - 1) % nn], LZ, 1) for n in range(nn)], axis=0)
    back[pl.ds(2 * R + 1, nd, stride=8), :] = jnp.zeros((nd, LX), f32)
    home = ship(back, got, s2, r2)
    out.wait_send()
    home.wait_recv()
    home.wait_send()


def solve_part(source, to_modes, walls, own):
    nn, nb = lax.axis_size("narrow"), lax.axis_size("wide")
    f32 = jnp.float32
    nd = nn * nb
    edge = np.zeros((LZ, LX, LX))
    for j in range(LZ):
        edge[j, :, j] = QXL
        edge[j, :, LZ + j] = QXF
    edge_h, edge_l = halves(edge.reshape(LZ // 2, 2 * LX, LX))
    slot = np.arange(LX) % LZ
    nu_lane = NU[slot][None]
    table, ex = fourier(nn * LX)
    spec = np.einsum("knx,ix->nik", table.reshape(-1, nn, LX), QX).reshape(nn * LX, nn * LX)
    turn, eb = fourier(nb)
    turn = np.kron(np.eye(LX // nb), turn)
    q_lane = np.zeros((8 + 2 * LX, LX))
    q_lane[0], q_lane[1], q_lane[2], q_lane[3] = QXL, QXF, QZL[slot], QZF[slot]
    q_lane[8:8 + LX] = (QXL ** 2)[:, None]
    q_lane[8 + LX:] = (QXL * QXF)[:, None]
    single = [MU[None], paired(QX.T), np.concatenate([edge_h, edge_l], axis=2), edge_h, nu_lane,
              np.broadcast_to(NU[slot][:, None], (LX, LX)), np.broadcast_to(MU[:, None], (LX, LX)), q_lane,
              *halves(spec), *halves(spec.T), *halves(turn), *halves(turn.T),
              np.broadcast_to(1 - eb[:, None] / 2, (nb, nn * LX)), ex[None]]
    consts = [jnp.asarray(a if a.dtype == ml_dtypes.bfloat16 else a.astype(np.float32)) for a in single]
    vmem, smem = (pl.BlockSpec(memory_space=m) for m in (pltpu.VMEM, pltpu.SMEM))
    dma = pltpu.SemaphoreType.DMA
    return pl.pallas_call(
        functools.partial(solve_kernel, nn, nb),
        out_shape=(jax.ShapeDtypeStruct((LZ, NY, LX), f32), jax.ShapeDtypeStruct((nd * 8, LX), f32)),
        in_specs=[vmem, vmem, vmem, smem] + [vmem] * len(consts),
        out_specs=(vmem, vmem),
        scratch_shapes=[
            pltpu.VMEM((LZ, NY, LX), f32), pltpu.VMEM((LZ, NY, LX), f32), pltpu.VMEM((NY, LX), f32), pltpu.VMEM((NY, LX), f32),
            pltpu.VMEM((nd * 8, LX), f32), pltpu.VMEM((nd * 8, LX), f32), pltpu.VMEM((nd * 8, LX), f32),
            dma, dma, dma, dma, dma,
        ],
        compiler_params=pltpu.CompilerParams(collective_id=1, has_side_effects=True, vmem_limit_bytes=56 * 1024 * 1024),
        name="modes_solve",
    )(source, to_modes, walls, own, *consts)


def last_kernel(fh, got, walls, from_modes, spacing, star_hbm, mu_row, xw, side_x, side_z, out_hbm,
                star, ph, press, across, load_sem, store_sem):
    f32 = jnp.float32
    loads = [pltpu.make_async_copy(star_hbm.at[c], star.at[c], load_sem.at[c]) for c in range(3)]
    for cp in loads:
        cp.start()
    nd = got.shape[0] // 8
    lane = lax.broadcasted_iota(jnp.int32, (nd, LX), 1)
    rim = got[pl.ds(2 * R, nd, stride=8), :]
    cols = []
    for r in range(R):
        a = jnp.where(lane < SLOT, rim if r == 0 else pltpu.roll(rim, LX - SLOT * r, 1), 0.0)
        high = a.astype(jnp.bfloat16).astype(f32)
        low = a - high
        cols.append(high + pltpu.roll(low, SLOT, 1) + pltpu.roll(high, 2 * SLOT, 1))
    cols = jnp.concatenate(cols, axis=0).astype(jnp.bfloat16)
    yb = [got[pl.ds(r, nd, stride=8), :] for r in range(R)]
    ya = [got[pl.ds(R + r, nd, stride=8), :] for r in range(R)]
    for r in range(R):
        across[0, pl.ds(r * nd, nd), :] = yb[r]
        across[1, pl.ds(r * nd, nd), :] = ya[r]
    for j in range(LZ):
        ph[1 + j] = mm(cols, side_x[:, j * LX:(j + 1) * LX])

    def chunk(k, _):
        rows = pl.ds(pl.multiple_of(k * 8, 8), 8)
        b, a = across[0, rows, :], across[1, rows, :]
        jump = (b - a, b + a)
        base = walls[rows, :] + mu_row[...]
        f = [(float(QZL[j]) * jump[j % 2] + (ph[1 + j, rows, :] - fh[j, rows, :])) * pl.reciprocal(base + float(NU[j]))
             for j in range(LZ)]
        x = from_cosines(f)
        for z in range(LZ):
            ph[1 + z, rows, :] = x[z]
        ph[0, rows, :] = x[0] - a
        ph[LZ + 1, rows, :] = x[LZ - 1] + b
        return 0

    lax.fori_loop(0, NY // 8, chunk, 0)
    m_high, m_low = split(from_modes[...])

    def modes(a):
        high, low = split(a)
        return mm(m_high, high) + mm(m_low, high) + mm(m_high, low)

    zero = jnp.zeros((8, LX), f32)
    for z in range(0, LZ + 2, 2):
        pair = []
        for k in range(2):
            high, low = split(ph[z + k])
            both = mm(jnp.concatenate([high, low], axis=1), xw[...])
            pair.append(both[:, :LX] + both[:, LX:])
        both = modes(jnp.concatenate(pair, axis=1))
        for k in range(2):
            press[z + k, pl.ds(0, 8), :] = zero
            press[z + k, pl.ds(8, NY), :] = both[:, k * LX:(k + 1) * LX]
            press[z + k, pl.ds(8 + NY, 8), :] = zero
    across[0] = modes(mm(cols, side_z[...]))
    for cp in loads:
        cp.wait()
    part = 64
    lane = lax.broadcasted_iota(jnp.int32, (part, LX), 1)

    def store(k):
        rows = pl.ds(pl.multiple_of(k * part * LZ, 8), part * LZ)
        return [pltpu.make_async_copy(star.at[c, rows], out_hbm.at[c, rows], store_sem.at[c, k]) for c in range(3)]

    def correct(k, _):
        at = pl.multiple_of(k * part, part)
        rim = across[0, pl.ds(at, part), :]
        slope = 0.05 * spacing[pl.ds(at, part), :]
        for z in range(LZ):
            p = press[1 + z, pl.ds(at + 8, part), :]
            east = jnp.where(lane == LX - 1, p + rim[:, z:z + 1], pltpu.roll(p, LX - 1, 1))
            west = jnp.where(lane == 0, p - rim[:, LZ + z:LZ + z + 1], pltpu.roll(p, 1, 1))
            up = press[1 + z, pl.ds(at + 9, part), :]
            down = press[1 + z, pl.ds(at + 7, part), :]
            north = press[2 + z, pl.ds(at + 8, part), :]
            south = press[z, pl.ds(at + 8, part), :]
            rows = pl.ds(at * LZ + z, part, stride=LZ)
            star[0, rows, :] = star[0, rows, :] - 0.05 * (east - west)
            star[1, rows, :] = star[1, rows, :] - slope * (up - down)
            star[2, rows, :] = star[2, rows, :] - 0.05 * (north - south)
        for cp in store(k):
            cp.start()
        return 0

    lax.fori_loop(0, NY // part, correct, 0)

    def finish(k, _):
        for cp in store(k):
            cp.wait()
        return 0

    lax.fori_loop(0, NY // part, finish, 0)


def last_part(fh, got, walls, from_modes, spacing, star):
    f32 = jnp.float32
    side_x = np.zeros((SLOT, LZ, LX))
    side_z = np.zeros((SLOT, LX))
    for j in range(LZ):
        side_x[j, j] = QXL
        side_x[LZ + j, j] = -QXF
    side_z[:LZ, :LZ] = QZ
    side_z[LZ:, LZ:SLOT] = QZ

    def stacked(a):
        high, low = halves(a)
        return jnp.asarray(np.concatenate([high, high, low, np.zeros_like(low)], axis=0))

    consts = [jnp.asarray(MU[None].astype(np.float32)), jnp.asarray(paired(QX)),
              stacked(side_x.reshape(SLOT, LZ * LX)), stacked(side_z)]
    vmem, any_ = (pl.BlockSpec(memory_space=m) for m in (pltpu.VMEM, pl.ANY))
    parts = NY // 64
    return pl.pallas_call(
        last_kernel,
        out_shape=jax.ShapeDtypeStruct((3, ROWS, LX), f32),
        in_specs=[vmem] * 5 + [any_] + [vmem] * 4,
        out_specs=any_,
        scratch_shapes=[
            pltpu.VMEM((3, ROWS, LX), f32), pltpu.VMEM((LZ + 2, NY, LX), f32), pltpu.VMEM((LZ + 2, NY + 16, LX), f32),
            pltpu.VMEM((2, NY, LX), f32), pltpu.SemaphoreType.DMA((3,)), pltpu.SemaphoreType.DMA((3, parts)),
        ],
        compiler_params=pltpu.CompilerParams(vmem_limit_bytes=56 * 1024 * 1024),
        name="synthesis_correct",
    )(fh, got, walls, from_modes, spacing, star, *consts)


def shards(velocity, inv_spacing, eigen_wall, to_modes, from_modes):
    star, source, walls = first_part(velocity, inv_spacing, eigen_wall)
    nn, nb = lax.axis_size("narrow"), lax.axis_size("wide")
    c_all = walls[:, 0, :3].reshape(nb, nn, 3).transpose(1, 0, 2).reshape(-1)
    me = lax.axis_index("narrow") * nb + lax.axis_index("wide")
    own = lax.dynamic_index_in_dim(c_all.reshape(-1, nn * nb), me, axis=1, keepdims=False)
    spread = jnp.broadcast_to(c_all[:, None], (NY, LX))
    fh, got = solve_part(source, to_modes, spread, own)
    spacing = jnp.broadcast_to(inv_spacing[:, None], (NY, LX))
    return last_part(fh, got, spread, from_modes, spacing, star).reshape(3, NY, LZ, LX)


def solution(mesh):
    in_specs = (P(None, None, "wide", "narrow"), P(), P(("narrow", "wide")), P(), P())
    out_specs = P(None, None, "wide", "narrow")
    return jax.shard_map(shards, mesh=mesh, in_specs=in_specs, out_specs=out_specs, check_vma=False)
```

```python
import functools
import math

import jax
import jax.numpy as jnp
import ml_dtypes
import numpy as np
from jax import lax
from jax.experimental import pallas as pl
from jax.experimental.pallas import tpu as pltpu
from jax.sharding import PartitionSpec as P

MESH = pl.DeviceIdType.MESH
LZ = 16
LX = 128
NY = 384
ROWS = NY * LZ
GROUPS = NY // LX


def split(a):
    high = a.astype(jnp.bfloat16)
    return high, (a - high.astype(jnp.float32)).astype(jnp.bfloat16)


def mm(a, b):
    return jnp.dot(a, b, preferred_element_type=jnp.float32)


def mm3(a, b_high, b_low):
    high, low = split(a)
    return mm(high, b_high) + mm(low, b_high) + mm(high, b_low)


def cosines(n):
    j = np.arange(n)[:, None]
    z = np.arange(n)[None, :]
    q = np.cos(np.pi * j * (z + 0.5) / n) * np.where(j == 0, math.sqrt(1 / n), math.sqrt(2 / n))
    return q, 2 - 2 * np.cos(np.pi * np.arange(n) / n)


def fourier(n):
    r = np.arange(n)[:, None]
    c = np.arange(n)[None, :]
    mid = n // 2
    k = np.where(r <= mid, r, r - mid)
    phase = (k * c % n) * (2 * np.pi / n)
    waves = np.where(r <= mid, np.cos(phase), np.sin(phase))
    weight = np.where((r == 0) | (r == mid), math.sqrt(1 / n), math.sqrt(2 / n))
    return waves * weight, 2 - 2 * np.cos(2 * np.pi * k[:, 0] / n)


def halves(a):
    a = np.asarray(a, np.float32)
    high = a.astype(ml_dtypes.bfloat16)
    return high, (a - high.astype(np.float32)).astype(ml_dtypes.bfloat16)


def paired(a):
    high, low = halves(a)
    return np.block([[high, low], [high, np.zeros_like(low)]])


QZ, NU = cosines(LZ)
QX, MU = cosines(LX)
QZL, QZF = QZ[:, -1], QZ[:, 0]
QXL, QXF = QX[:, -1], QX[:, 0]
SLOT = 2 * LZ
R = 3


def to_cosines(x):
    n = len(x)
    out = [None] * n
    e = [x[z] + x[n - 1 - z] for z in range(n // 2)]
    o = [x[z] - x[n - 1 - z] for z in range(n // 2)]
    ee = [e[z] + e[n // 2 - 1 - z] for z in range(n // 4)]
    eo = [e[z] - e[n // 2 - 1 - z] for z in range(n // 4)]
    for j in range(n):
        part = o if j % 2 else (eo if j % 4 else ee)
        out[j] = sum(float(QZ[j, z]) * part[z] for z in range(len(part)))
    return out


def from_cosines(f):
    n = len(f)
    even, out = [None] * (n // 2), [None] * n
    for z in range(n // 4):
        a = sum(float(QZ[j, z]) * f[j] for j in range(0, n, 4))
        b = sum(float(QZ[j, z]) * f[j] for j in range(2, n, 4))
        even[z], even[n // 2 - 1 - z] = a + b, a - b
    for z in range(n // 2):
        odd = sum(float(QZ[j, z]) * f[j] for j in range(1, n, 2))
        out[z], out[n - 1 - z] = even[z] + odd, even[z] - odd
    return out


def front_kernel(nn, nb, v_hbm, spacing, eig, modes_hbm, xw_hbm, edge_hl_hbm, edge_h_hbm, spec_h_hbm, spec_l_hbm,
                 back_h_hbm, back_l_hbm, mu_row, nu_lane, nu_row, mu_col, q_lane, turn_h, turn_l, unturn_h, unturn_l,
                 cos_b, ex_row, star_hbm, walls, fh, got,
                 v, star, rim, zsend, zrecv, xsend, xrecv, s2send, s2recv, x0send, x0recv,
                 load_sem, store_sem, z_ss, z_rs, x_ss, x_rs, s2_ss, s2_rs, x0_ss, x0_rs, e_ss, e_rs,
                 source, tiles, gz, gh, zl, zf, send, recv, back, s1, r1, s2, r2,
                 to_modes, xw, edge_hl, edge_h, spec_h, spec_l, back_h, back_l, const_sem):
    large = ((modes_hbm, to_modes), (xw_hbm, xw), (edge_hl_hbm, edge_hl), (edge_h_hbm, edge_h),
             (spec_h_hbm, spec_h), (spec_l_hbm, spec_l), (back_h_hbm, back_h), (back_l_hbm, back_l))
    me_n = lax.axis_index("narrow")
    me_b = lax.axis_index("wide")
    ring = nb // 4
    layer = me_b // ring
    spot = lax.rem(me_b, ring)
    up = (me_n, lax.rem(me_b + 1, nb))
    down = (me_n, lax.rem(me_b + nb - 1, nb))
    right = (lax.rem(me_n + 1, nn), me_b)
    left = (lax.rem(me_n + nn - 1, nn), me_b)

    loads = [pltpu.make_async_copy(v_hbm.at[c], v.at[c, pl.ds(LZ, ROWS)], load_sem.at[c]) for c in range(3)]
    for c in (2, 0, 1):
        loads[c].start()

    fetches = [pltpu.make_async_copy(h, m, const_sem.at[k]) for k, (h, m) in enumerate(large)]
    for cp in fetches:
        cp.start()
    barrier = pltpu.get_barrier_semaphore()
    narrow_peers = [(lax.rem(me_n + k, nn), me_b) for k in range(1, nn)]
    spot_peers = [(me_n, layer * ring + lax.rem(spot + k, ring)) for k in range(1, ring)]
    layer_peers = [(me_n, lax.rem(layer + k, 4) * ring + spot) for k in range(1, 4)]
    greeted = [up, down] + narrow_peers + spot_peers + layer_peers
    for peer in greeted:
        pl.semaphore_signal(barrier, inc=1, device_id=peer, device_id_type=MESH)

    zero = jnp.zeros((LZ, LX), jnp.float32)
    for c in range(3):
        v[c, pl.ds(0, LZ), :] = zero
        v[c, pl.ds(LZ + ROWS, LZ), :] = zero
        star[c, pl.ds(0, LZ), :] = zero
        star[c, pl.ds(LZ + ROWS, LZ), :] = zero
    each = NY // (nn * nb)
    me = me_n * nb + me_b
    which = lax.broadcasted_iota(jnp.int32, (8, LX), 0)
    values = jnp.zeros((8, LX), jnp.float32)
    for k in range(each):
        values = jnp.where(which == k, eig[k], values)
    tiles[pl.ds(pl.multiple_of(me * 8, 8), 8), :] = values
    pl.semaphore_wait(barrier, len(greeted))

    def share(peers, at, count, stage):
        for k, peer in enumerate(peers):
            pltpu.make_async_remote_copy(
                src_ref=tiles.at[pl.ds(pl.multiple_of(at * 8, 8), count * 8)], dst_ref=tiles.at[pl.ds(pl.multiple_of(at * 8, 8), count * 8)],
                send_sem=e_ss.at[stage], recv_sem=e_rs.at[stage], device_id=peer, device_id_type=MESH).start()

    def share_wait(peers, count, stage):
        n = len(peers) * count
        w = pltpu.make_async_remote_copy(
            src_ref=tiles.at[pl.ds(0, n * 8)], dst_ref=tiles.at[pl.ds(0, n * 8)],
            send_sem=e_ss.at[stage], recv_sem=e_rs.at[stage], device_id=peers[0], device_id_type=MESH)
        w.wait_send()
        w.wait_recv()

    def remote(src_ref, dst_ref, ss, rs, peer):
        return pltpu.make_async_remote_copy(src_ref=src_ref, dst_ref=dst_ref, send_sem=ss, recv_sem=rs,
                                            device_id=peer, device_id_type=MESH)

    lane = lax.broadcasted_iota(jnp.int32, (LZ, LX), 1)
    level = lax.broadcasted_iota(jnp.int32, (LZ, LX), 0)

    def pack(ref, c, g):
        def step(yy, carry):
            last, first = carry
            plane = ref[c, pl.ds(pl.multiple_of(LZ + (g * LX + yy) * LZ, LZ), LZ), :]
            turned = pltpu.roll(plane, lax.rem(yy + 1, LX), 1)
            last = jnp.where(lane == yy, turned, last)
            first = jnp.where(lane == lax.rem(yy + 1, LX), turned, first)
            return last, first
        last, first = lax.fori_loop(0, LX, step, (zero, zero), unroll=16)
        return last, pltpu.roll(first, LX - 1, 1)

    share(spot_peers, me, 1, 0)
    zcopies, xcopies = [], []
    for c in (2, 0, 1):
        loads[c].wait()
        zsend[0, c] = v[c, pl.ds(LZ + LZ - 1, NY, stride=LZ), :]
        zsend[1, c] = v[c, pl.ds(LZ, NY, stride=LZ), :]
        for side, peer in ((0, up), (1, down)):
            cp = remote(zsend.at[side, c], zrecv.at[side, c], z_ss.at[side, c], z_rs.at[side, c], peer)
            cp.start()
            zcopies.append(cp)
        for g in range(GROUPS):
            last, first = pack(v, c, g)
            xsend[0, c, g] = last
            xsend[1, c, g] = first
        for side, peer in ((0, right), (1, left)):
            cp = remote(xsend.at[side, c], xrecv.at[side, c], x_ss.at[side, c], x_rs.at[side, c], peer)
            cp.start()
            xcopies.append(cp)

    share_wait(spot_peers, 1, 0)
    share(layer_peers, me_n * nb + layer * ring, ring, 1)
    for cp in xcopies:
        cp.wait_recv()
    even = lax.rem(lane, 2) == 0

    def interleave(east, west):
        west = pltpu.roll(west, 1, 1)
        return jnp.where(even, east, west), jnp.where(even, west, east)

    for c in range(3):
        for g in range(GROUPS):
            rim[c, g, 0], rim[c, g, 1] = interleave(xrecv[1, c, g], xrecv[0, c, g])

    def predict_plane(y, odd):
        g = y // LX
        yy = lax.rem(y, LX)
        base = pl.multiple_of(LZ + y * LZ, LZ)
        s = spacing[y]
        centre = [v[c, pl.ds(base, LZ), :] for c in range(3)]
        a_e = 0.05 - 0.05 * centre[0]
        a_w = 0.05 + 0.05 * centre[0]
        a_n = jnp.where(level == LZ - 1, 0.0, 0.05 - 0.05 * centre[2])
        a_s = jnp.where(level == 0, 0.0, 0.05 + 0.05 * centre[2])
        curve = 0.05 * s * s
        slope = (0.05 * s) * centre[1]
        a_u = curve - slope
        a_l = curve + slope
        a_c = 0.8 - 2.0 * curve
        for c in range(3):
            f = centre[c]
            upper = v[c, pl.ds(base + LZ, LZ), :]
            lower = v[c, pl.ds(base - LZ, LZ), :]
            north = v[c, pl.ds(base + 1, LZ), :]
            south = v[c, pl.ds(base - 1, LZ), :]
            ends = pltpu.roll(rim[c, g, odd], LX - 1 - yy, 1)
            east = jnp.where(lane == LX - 1, ends, pltpu.roll(f, LX - 1, 1))
            west = jnp.where(lane == 0, ends, pltpu.roll(f, 1, 1))
            star[c, pl.ds(base, LZ), :] = (
                a_c * f + a_e * east + a_w * west + (a_n * north + a_s * south) + (a_u * upper + a_l * lower))

    def predict_pair(k, _):
        predict_plane(2 * k, 0)
        predict_plane(2 * k + 1, 1)
        return 0

    lax.fori_loop(0, NY // 2, predict_pair, 0, unroll=8)

    share_wait(layer_peers, ring, 1)
    share(narrow_peers, me_n * nb, nb, 2)
    for cp in zcopies:
        cp.wait_recv()
    part = 96
    for c in (2, 0, 1):
        for k in range(NY // part):
            hi = LZ + k * part * LZ + LZ - 1
            lo = LZ + k * part * LZ
            rows = pl.ds(k * part, part)
            top = star[c, pl.ds(hi, part, stride=LZ), :] + zrecv[1, c, rows, :] * (
                0.05 - 0.05 * v[2, pl.ds(hi, part, stride=LZ), :])
            low = star[c, pl.ds(lo, part, stride=LZ), :] + zrecv[0, c, rows, :] * (
                0.05 + 0.05 * v[2, pl.ds(lo, part, stride=LZ), :])
            star[c, pl.ds(hi, part, stride=LZ), :] = top
            star[c, pl.ds(lo, part, stride=LZ), :] = low
            if c == 2:
                s2send[0, rows, :] = top
                s2send[1, rows, :] = low
        if c == 2:
            s2copies = [remote(s2send.at[side], s2recv.at[side], s2_ss.at[side], s2_rs.at[side], peer)
                        for side, peer in ((0, up), (1, down))]
            for cp in s2copies:
                cp.start()
        if c == 0:
            for g in range(GROUPS):
                last, first = pack(star, 0, g)
                x0send[0, g] = last
                x0send[1, g] = first
            x0copies = [remote(x0send.at[side], x0recv.at[side], x0_ss.at[side], x0_rs.at[side], peer)
                        for side, peer in ((0, right), (1, left))]
            for cp in x0copies:
                cp.start()
    stores = [pltpu.make_async_copy(star.at[c, pl.ds(LZ, ROWS)], star_hbm.at[c], store_sem.at[c]) for c in range(3)]
    for cp in stores:
        cp.start()
    for cp in x0copies:
        cp.wait_recv()
    for g in range(GROUPS):
        rim[0, g, 0], rim[0, g, 1] = interleave(x0recv[1, g], x0recv[0, g])

    def diverge_plane(y, odd):
        g = y // LX
        yy = lax.rem(y, LX)
        base = pl.multiple_of(LZ + y * LZ, LZ)
        s = 5.0 * spacing[y]
        f = star[0, pl.ds(base, LZ), :]
        ends = pltpu.roll(rim[0, g, odd], LX - 1 - yy, 1)
        east = jnp.where(lane == LX - 1, ends, pltpu.roll(f, LX - 1, 1))
        west = jnp.where(lane == 0, ends, pltpu.roll(f, 1, 1))
        north = jnp.where(level == LZ - 1, 0.0, star[2, pl.ds(base + 1, LZ), :])
        south = jnp.where(level == 0, 0.0, star[2, pl.ds(base - 1, LZ), :])
        rise = star[1, pl.ds(base + LZ, LZ), :] - star[1, pl.ds(base - LZ, LZ), :]
        source[pl.ds(y, LZ, stride=NY), :] = 5.0 * ((east - west) + (north - south)) + s * rise

    def diverge_pair(k, _):
        diverge_plane(2 * k, 0)
        diverge_plane(2 * k + 1, 1)
        return 0

    lax.fori_loop(0, NY // 2, diverge_pair, 0, unroll=8)

    f32 = jnp.float32
    nd = nn * nb
    for cp in fetches:
        cp.wait()
    t_high, t_low = split(to_modes[...])

    def slabs(pair):
        s_high, s_low = split(jnp.concatenate([source[pl.ds(z * NY, NY), :] for z in pair], axis=1))
        modal = mm(t_high, s_high) + mm(t_low, s_high) + mm(t_high, s_low)
        for k, z in enumerate(pair):
            high, low = split(modal[:, k * LX:(k + 1) * LX])
            both = mm(jnp.concatenate([high, low], axis=1), xw[...])
            gz[z] = both[:, :LX] + both[:, LX:]

    for z in range(1, LZ - 1, 2):
        slabs((z, z + 1))
    for cp in s2copies:
        cp.wait_recv()
    low, top = pl.ds(0, NY), pl.ds((LZ - 1) * NY, NY)
    source[low, :] = source[low, :] - 5.0 * s2recv[0]
    source[top, :] = source[top, :] + 5.0 * s2recv[1]
    slabs((0, LZ - 1))
    share_wait(narrow_peers, nb, 2)
    each = NY // nd
    for k in range(each):
        walls[pl.ds(k, nd, stride=each), :] = tiles[pl.ds(k, nd, stride=8), :]

    def chunk(k, _):
        rows = pl.ds(pl.multiple_of(k * 8, 8), 8)
        f = to_cosines([gz[z, rows, :] for z in range(LZ)])
        base = walls[rows, :] + mu_row[...]
        sums = [None, None]
        for j in range(LZ):
            fh[j, rows, :] = f[j]
            g = f[j] * pl.reciprocal(base + float(NU[j]))
            gh[j, rows, :] = g
            term = float(QZL[j]) * g
            sums[j % 2] = term if sums[j % 2] is None else sums[j % 2] + term
        zl[rows, :] = sums[0] + sums[1]
        zf[rows, :] = sums[0] - sums[1]
        return 0

    lax.fori_loop(0, NY // 8, chunk, 0)
    edge = jnp.zeros((NY, LX), f32)
    for j in range(0, LZ, 2):
        high, low = split(jnp.concatenate([gh[j], gh[j + 1]], axis=1))
        both = mm(high, edge_hl[j // 2])
        edge = edge + both[:, :LX] + both[:, LX:] + mm(low, edge_h[j // 2])
    packed = edge[:nd]
    for r in range(R):
        rows = pl.ds(r * nd, nd)
        send[pl.ds(r, nd, stride=8), :] = zl[rows, :]
        send[pl.ds(R + r, nd, stride=8), :] = zf[rows, :]
        if r:
            packed = packed + pltpu.roll(edge[r * nd:(r + 1) * nd], SLOT * r, 1)
    send[pl.ds(2 * R, nd, stride=8), :] = packed
    send[pl.ds(2 * R + 1, nd, stride=8), :] = jnp.zeros((nd, LX), f32)

    def ship(src, dst, ss, rs):
        def go(k, _):
            d = me + k
            d = jnp.where(d >= nd, d - nd, d)
            pltpu.make_async_remote_copy(
                src_ref=src.at[pl.ds(pl.multiple_of(d * 8, 8), 8)], dst_ref=dst.at[pl.ds(pl.multiple_of(me * 8, 8), 8)],
                send_sem=ss, recv_sem=rs, device_id=d, device_id_type=pl.DeviceIdType.LOGICAL).start()
            return 0
        lax.fori_loop(1, nd, go, 0, unroll=8)
        mine = pl.ds(pl.multiple_of(me * 8, 8), 8)
        dst[mine, :] = src[mine, :]
        most = pl.ds(0, (nd - 1) * 8)
        return pltpu.make_async_remote_copy(src_ref=src.at[most], dst_ref=dst.at[most], send_sem=ss, recv_sem=rs,
                                            device_id=(me_n, me_b), device_id_type=MESH)

    out = ship(send, recv, s1, r1)

    own = [walls[pl.ds(r * nd + me, 1), :] for r in range(R)]
    lane = lax.broadcasted_iota(jnp.int32, (1, LX), 1)
    owner_lane = jnp.where(lane < SLOT, own[0], jnp.where(lane < 2 * SLOT, own[1], own[2]))
    rowid = lax.broadcasted_iota(jnp.int32, (LX, LX), 0)
    owner_row = jnp.where(rowid < SLOT, own[0], jnp.where(rowid < 2 * SLOT, own[1], own[2]))
    low_half = lax.rem(lane, SLOT) < LZ
    d_rows = pl.reciprocal(owner_row + nu_row[...] + mu_row[...])
    d_cols = pl.reciprocal(owner_lane + nu_lane[...] + mu_col[...])
    qxl, qxf = q_lane[0:1], q_lane[1:2]
    qzl = jnp.where(low_half, q_lane[2:3], 0.0)
    qzf = jnp.where(low_half, q_lane[3:4], 0.0)
    hll = jnp.sum(d_cols * q_lane[8:8 + LX], axis=0, keepdims=True)
    hlf = jnp.sum(d_cols * q_lane[8 + LX:8 + 2 * LX], axis=0, keepdims=True)
    l0, l1, l2 = (1.0 / (1 + 2 * hll - 2 * hlf), 1.0 / (1 + 2 * hll), 1.0 / (1 + 2 * hll + 2 * hlf))
    k0, k1, k2 = (0.25 * (l0 + 2 * l1 + l2), 0.25 * (l0 - l2), 0.25 * (l0 - 2 * l1 + l2))
    dr_h, dr_l = split(d_rows)
    dc_h, dc_l = split(d_cols)
    scale = []
    for r in range(R):
        gll = jnp.zeros_like(ex_row[...])
        glf = jnp.zeros_like(ex_row[...])
        base = jnp.concatenate([own[r]] * nn, axis=1) + ex_row[...]
        for j in range(LZ):
            g = 1.0 / (base + float(NU[j]))
            gll = gll + float(QZL[j] ** 2) * g
            glf = glf + float(QZL[j] * QZF[j]) * g
        scale.append(1.0 / (1 + 2 * gll - 2 * glf * cos_b[...]))
    scale = jnp.concatenate(scale, axis=0)

    def coupled(a):
        return [k0 * a[n] + k1 * (a[(n + 1) % nn] + a[(n - 1) % nn]) + k2 * a[(n + 2) % nn] for n in range(nn)]

    def ahead(a):
        return pltpu.roll(a, nb - 1, 0)

    def behind(a):
        return pltpu.roll(a, 1, 0)

    def blocks(a):
        return [a[n * nb:(n + 1) * nb] for n in range(nn)]

    out.wait_recv()
    x = blocks(recv[pl.ds(2 * R, nd, stride=8), :])
    t = coupled([jnp.where(low_half, x[n] - pltpu.roll(x[(n + 1) % nn], LX - LZ, 1), 0.0) for n in range(nn)])
    big = jnp.concatenate([qzl * t[n] - qzf * ahead(t[n]) for n in range(nn)], axis=0)
    lines = []
    for r in range(R):
        mine = (lane >= SLOT * r) & (lane < SLOT * (r + 1))
        td = blocks(mm3(jnp.where(mine, big, 0.0), dr_h, dr_l))
        last = blocks(recv[pl.ds(r, nd, stride=8), :])
        first = blocks(recv[pl.ds(R + r, nd, stride=8), :])
        lines.append(jnp.concatenate(
            [last[n] - ahead(first[n]) - (qxl * td[n] - qxf * td[(n - 1) % nn]) for n in range(nn)], axis=1))
    s = mm3(jnp.concatenate(lines, axis=0), spec_h[...], spec_l[...])
    s = jnp.concatenate([s, jnp.zeros((LX - R * nb, nn * LX), f32)], axis=0)
    s_h, s_l = split(s)
    s = mm(turn_h[...], s_h) + mm(turn_l[...], s_h) + mm(turn_h[...], s_l)
    s = jnp.concatenate([s[:R * nb] * scale, s[R * nb:]], axis=0)
    s_h, s_l = split(s)
    s = mm(unturn_h[...], s_h) + mm(unturn_l[...], s_h) + mm(unturn_h[...], s_l)
    y = mm3(s[:R * nb], back_h[...], back_l[...])
    zsum = jnp.zeros((nd, LX), f32)
    for r in range(R):
        yr = [y[r * nb:(r + 1) * nb, n * LX:(n + 1) * LX] for n in range(nn)]
        back[pl.ds(r, nd, stride=8), :] = jnp.concatenate(yr, axis=0)
        back[pl.ds(R + r, nd, stride=8), :] = jnp.concatenate([behind(a) for a in yr], axis=0)
        mine = (lane >= SLOT * r) & (lane < SLOT * (r + 1))
        ends = jnp.concatenate([qxl * yr[n] - qxf * yr[(n + 1) % nn] for n in range(nn)], axis=0)
        zsum = zsum + jnp.where(mine, mm3(ends, dc_h, dc_l), 0.0)
    zs = blocks(zsum)
    u = coupled([qzl * zs[n] - qzf * behind(zs[n]) for n in range(nn)])
    w = [jnp.where(low_half, t[n] - u[n], 0.0) for n in range(nn)]
    back[pl.ds(2 * R, nd, stride=8), :] = jnp.concatenate(
        [w[n] + pltpu.roll(w[(n - 1) % nn], LZ, 1) for n in range(nn)], axis=0)
    back[pl.ds(2 * R + 1, nd, stride=8), :] = jnp.zeros((nd, LX), f32)
    home = ship(back, got, s2, r2)
    out.wait_send()
    home.wait_recv()
    home.wait_send()
    for cp in zcopies + xcopies + s2copies + x0copies:
        cp.wait_send()
    for cp in stores:
        cp.wait()


def front_part(velocity, inv_spacing, eigen_wall, to_modes):
    nn, nb = lax.axis_size("narrow"), lax.axis_size("wide")
    f32 = jnp.float32
    nd = nn * nb
    edge = np.zeros((LZ, LX, LX))
    for j in range(LZ):
        edge[j, :, j] = QXL
        edge[j, :, LZ + j] = QXF
    edge_h, edge_l = halves(edge.reshape(LZ // 2, 2 * LX, LX))
    slot = np.arange(LX) % LZ
    nu_lane = NU[slot][None]
    table, ex = fourier(nn * LX)
    spec = np.einsum("knx,ix->nik", table.reshape(-1, nn, LX), QX).reshape(nn * LX, nn * LX)
    turn, eb = fourier(nb)
    turn = np.kron(np.eye(LX // nb), turn)
    q_lane = np.zeros((8 + 2 * LX, LX))
    q_lane[0], q_lane[1], q_lane[2], q_lane[3] = QXL, QXF, QZL[slot], QZF[slot]
    q_lane[8:8 + LX] = (QXL ** 2)[:, None]
    q_lane[8 + LX:] = (QXL * QXF)[:, None]
    big = [paired(QX.T), np.concatenate([edge_h, edge_l], axis=2), edge_h, *halves(spec), *halves(spec.T)]
    small = [MU[None], nu_lane, np.broadcast_to(NU[slot][:, None], (LX, LX)), np.broadcast_to(MU[:, None], (LX, LX)), q_lane,
             *halves(turn), *halves(turn.T), np.broadcast_to(1 - eb[:, None] / 2, (nb, nn * LX)), ex[None]]
    consts = [jnp.asarray(a if a.dtype == ml_dtypes.bfloat16 else a.astype(np.float32)) for a in big + small]
    any_, vmem, smem = (pl.BlockSpec(memory_space=m) for m in (pl.ANY, pltpu.VMEM, pltpu.SMEM))
    dma = pltpu.SemaphoreType.DMA
    return pl.pallas_call(
        functools.partial(front_kernel, nn, nb),
        out_shape=(jax.ShapeDtypeStruct((3, ROWS, LX), f32), jax.ShapeDtypeStruct((NY, LX), f32),
                   jax.ShapeDtypeStruct((LZ, NY, LX), f32), jax.ShapeDtypeStruct((nd * 8, LX), f32)),
        in_specs=[any_, smem, smem] + [any_] * (1 + len(big)) + [vmem] * len(small),
        out_specs=(any_, vmem, vmem, vmem),
        scratch_shapes=[
            pltpu.VMEM((3, ROWS + 2 * LZ, LX), f32), pltpu.VMEM((3, ROWS + 2 * LZ, LX), f32), pltpu.VMEM((3, GROUPS, 2, LZ, LX), f32),
            pltpu.VMEM((2, 3, NY, LX), f32), pltpu.VMEM((2, 3, NY, LX), f32),
            pltpu.VMEM((2, 3, GROUPS, LZ, LX), f32), pltpu.VMEM((2, 3, GROUPS, LZ, LX), f32),
            pltpu.VMEM((2, NY, LX), f32), pltpu.VMEM((2, NY, LX), f32),
            pltpu.VMEM((2, GROUPS, LZ, LX), f32), pltpu.VMEM((2, GROUPS, LZ, LX), f32),
            dma((3,)), dma((3,)), dma((2, 3)), dma((2, 3)), dma((2, 3)), dma((2, 3)),
            dma((2,)), dma((2,)), dma((2,)), dma((2,)), dma((3,)), dma((3,)),
            pltpu.VMEM((LZ * NY, LX), f32), pltpu.VMEM((nd * 8, LX), f32),
            pltpu.VMEM((LZ, NY, LX), f32), pltpu.VMEM((LZ, NY, LX), f32), pltpu.VMEM((NY, LX), f32), pltpu.VMEM((NY, LX), f32),
            pltpu.VMEM((nd * 8, LX), f32), pltpu.VMEM((nd * 8, LX), f32), pltpu.VMEM((nd * 8, LX), f32),
            dma, dma, dma, dma,
            pltpu.VMEM((NY, NY), f32), *[pltpu.VMEM(a.shape, jnp.bfloat16) for a in big], dma((1 + len(big),)),
        ],
        compiler_params=pltpu.CompilerParams(collective_id=0, has_side_effects=True, vmem_limit_bytes=60 * 1024 * 1024),
        name="predict_solve",
    )(velocity.reshape(3, ROWS, LX), inv_spacing, eigen_wall, to_modes, *consts)


def last_kernel(fh, got, walls, from_modes, spacing, star_hbm, mu_row, xw, side_x, side_z, out_hbm,
                star, ph, press, across, load_sem, store_sem):
    f32 = jnp.float32
    loads = [pltpu.make_async_copy(star_hbm.at[c], star.at[c], load_sem.at[c]) for c in range(3)]
    for cp in loads:
        cp.start()
    nd = got.shape[0] // 8
    lane = lax.broadcasted_iota(jnp.int32, (nd, LX), 1)
    rim = got[pl.ds(2 * R, nd, stride=8), :]
    cols = []
    for r in range(R):
        a = jnp.where(lane < SLOT, rim if r == 0 else pltpu.roll(rim, LX - SLOT * r, 1), 0.0)
        high = a.astype(jnp.bfloat16).astype(f32)
        low = a - high
        cols.append(high + pltpu.roll(low, SLOT, 1) + pltpu.roll(high, 2 * SLOT, 1))
    cols = jnp.concatenate(cols, axis=0).astype(jnp.bfloat16)
    yb = [got[pl.ds(r, nd, stride=8), :] for r in range(R)]
    ya = [got[pl.ds(R + r, nd, stride=8), :] for r in range(R)]
    for r in range(R):
        across[0, pl.ds(r * nd, nd), :] = yb[r]
        across[1, pl.ds(r * nd, nd), :] = ya[r]
    for j in range(LZ):
        ph[1 + j] = mm(cols, side_x[:, j * LX:(j + 1) * LX])

    def chunk(k, _):
        rows = pl.ds(pl.multiple_of(k * 8, 8), 8)
        b, a = across[0, rows, :], across[1, rows, :]
        jump = (b - a, b + a)
        base = walls[rows, :] + mu_row[...]
        f = [(float(QZL[j]) * jump[j % 2] + (ph[1 + j, rows, :] - fh[j, rows, :])) * pl.reciprocal(base + float(NU[j]))
             for j in range(LZ)]
        x = from_cosines(f)
        for z in range(LZ):
            ph[1 + z, rows, :] = x[z]
        ph[0, rows, :] = x[0] - a
        ph[LZ + 1, rows, :] = x[LZ - 1] + b
        return 0

    lax.fori_loop(0, NY // 8, chunk, 0)
    m_high, m_low = split(from_modes[...])

    def modes(a):
        high, low = split(a)
        return mm(m_high, high) + mm(m_low, high) + mm(m_high, low)

    zero = jnp.zeros((8, LX), f32)
    for z in range(0, LZ + 2, 2):
        pair = []
        for k in range(2):
            high, low = split(ph[z + k])
            both = mm(jnp.concatenate([high, low], axis=1), xw[...])
            pair.append(both[:, :LX] + both[:, LX:])
        both = modes(jnp.concatenate(pair, axis=1))
        for k in range(2):
            press[z + k, pl.ds(0, 8), :] = zero
            press[z + k, pl.ds(8, NY), :] = both[:, k * LX:(k + 1) * LX]
            press[z + k, pl.ds(8 + NY, 8), :] = zero
    across[0] = modes(mm(cols, side_z[...]))
    for cp in loads:
        cp.wait()
    part = 64
    lane = lax.broadcasted_iota(jnp.int32, (part, LX), 1)

    def store(k):
        rows = pl.ds(pl.multiple_of(k * part * LZ, 8), part * LZ)
        return [pltpu.make_async_copy(star.at[c, rows], out_hbm.at[c, rows], store_sem.at[c, k]) for c in range(3)]

    def correct(k, _):
        at = pl.multiple_of(k * part, part)
        rim = across[0, pl.ds(at, part), :]
        slope = 0.05 * spacing[pl.ds(at, part), :]
        for z in range(LZ):
            p = press[1 + z, pl.ds(at + 8, part), :]
            east = jnp.where(lane == LX - 1, p + rim[:, z:z + 1], pltpu.roll(p, LX - 1, 1))
            west = jnp.where(lane == 0, p - rim[:, LZ + z:LZ + z + 1], pltpu.roll(p, 1, 1))
            up = press[1 + z, pl.ds(at + 9, part), :]
            down = press[1 + z, pl.ds(at + 7, part), :]
            north = press[2 + z, pl.ds(at + 8, part), :]
            south = press[z, pl.ds(at + 8, part), :]
            rows = pl.ds(at * LZ + z, part, stride=LZ)
            star[0, rows, :] = star[0, rows, :] - 0.05 * (east - west)
            star[1, rows, :] = star[1, rows, :] - slope * (up - down)
            star[2, rows, :] = star[2, rows, :] - 0.05 * (north - south)
        for cp in store(k):
            cp.start()
        return 0

    lax.fori_loop(0, NY // part, correct, 0)

    def finish(k, _):
        for cp in store(k):
            cp.wait()
        return 0

    lax.fori_loop(0, NY // part, finish, 0)


def last_part(fh, got, walls, from_modes, spacing, star):
    f32 = jnp.float32
    side_x = np.zeros((SLOT, LZ, LX))
    side_z = np.zeros((SLOT, LX))
    for j in range(LZ):
        side_x[j, j] = QXL
        side_x[LZ + j, j] = -QXF
    side_z[:LZ, :LZ] = QZ
    side_z[LZ:, LZ:SLOT] = QZ

    def stacked(a):
        high, low = halves(a)
        return jnp.asarray(np.concatenate([high, high, low, np.zeros_like(low)], axis=0))

    consts = [jnp.asarray(MU[None].astype(np.float32)), jnp.asarray(paired(QX)),
              stacked(side_x.reshape(SLOT, LZ * LX)), stacked(side_z)]
    vmem, any_ = (pl.BlockSpec(memory_space=m) for m in (pltpu.VMEM, pl.ANY))
    parts = NY // 64
    return pl.pallas_call(
        last_kernel,
        out_shape=jax.ShapeDtypeStruct((3, ROWS, LX), f32),
        in_specs=[vmem] * 5 + [any_] + [vmem] * 4,
        out_specs=any_,
        scratch_shapes=[
            pltpu.VMEM((3, ROWS, LX), f32), pltpu.VMEM((LZ + 2, NY, LX), f32), pltpu.VMEM((LZ + 2, NY + 16, LX), f32),
            pltpu.VMEM((2, NY, LX), f32), pltpu.SemaphoreType.DMA((3,)), pltpu.SemaphoreType.DMA((3, parts)),
        ],
        compiler_params=pltpu.CompilerParams(vmem_limit_bytes=56 * 1024 * 1024),
        name="synthesis_correct",
    )(fh, got, walls, from_modes, spacing, star, *consts)


def shards(velocity, inv_spacing, eigen_wall, to_modes, from_modes):
    star, walls, fh, got = front_part(velocity, inv_spacing, eigen_wall, to_modes)
    spacing = jnp.broadcast_to(inv_spacing[:, None], (NY, LX))
    return last_part(fh, got, walls, from_modes, spacing, star).reshape(3, NY, LZ, LX)


def solution(mesh):
    in_specs = (P(None, None, "wide", "narrow"), P(), P(("narrow", "wide")), P(), P())
    out_specs = P(None, None, "wide", "narrow")
    return jax.shard_map(shards, mesh=mesh, in_specs=in_specs, out_specs=out_specs, check_vma=False)
```

```python
import functools
import math

import jax
import jax.numpy as jnp
import ml_dtypes
import numpy as np
from jax import lax
from jax.experimental import pallas as pl
from jax.experimental.pallas import tpu as pltpu
from jax.sharding import PartitionSpec as P

MESH = pl.DeviceIdType.MESH
LZ = 16
LX = 128
NY = 384
ROWS = NY * LZ
GROUPS = NY // LX


def split(a):
    high = a.astype(jnp.bfloat16)
    return high, (a - high.astype(jnp.float32)).astype(jnp.bfloat16)


def mm(a, b):
    return jnp.dot(a, b, preferred_element_type=jnp.float32)


def mm3(a, b_high, b_low):
    high, low = split(a)
    return mm(high, b_high) + mm(low, b_high) + mm(high, b_low)


def cosines(n):
    j = np.arange(n)[:, None]
    z = np.arange(n)[None, :]
    q = np.cos(np.pi * j * (z + 0.5) / n) * np.where(j == 0, math.sqrt(1 / n), math.sqrt(2 / n))
    return q, 2 - 2 * np.cos(np.pi * np.arange(n) / n)


def fourier(n):
    r = np.arange(n)[:, None]
    c = np.arange(n)[None, :]
    mid = n // 2
    k = np.where(r <= mid, r, r - mid)
    phase = (k * c % n) * (2 * np.pi / n)
    waves = np.where(r <= mid, np.cos(phase), np.sin(phase))
    weight = np.where((r == 0) | (r == mid), math.sqrt(1 / n), math.sqrt(2 / n))
    return waves * weight, 2 - 2 * np.cos(2 * np.pi * k[:, 0] / n)


def halves(a):
    a = np.asarray(a, np.float32)
    high = a.astype(ml_dtypes.bfloat16)
    return high, (a - high.astype(np.float32)).astype(ml_dtypes.bfloat16)


def paired(a):
    high, low = halves(a)
    return np.block([[high, low], [high, np.zeros_like(low)]])


QZ, NU = cosines(LZ)
QX, MU = cosines(LX)
QZL, QZF = QZ[:, -1], QZ[:, 0]
QXL, QXF = QX[:, -1], QX[:, 0]
SLOT = 2 * LZ
R = 3


def to_cosines(x):
    n = len(x)
    out = [None] * n
    e = [x[z] + x[n - 1 - z] for z in range(n // 2)]
    o = [x[z] - x[n - 1 - z] for z in range(n // 2)]
    ee = [e[z] + e[n // 2 - 1 - z] for z in range(n // 4)]
    eo = [e[z] - e[n // 2 - 1 - z] for z in range(n // 4)]
    for j in range(n):
        part = o if j % 2 else (eo if j % 4 else ee)
        out[j] = sum(float(QZ[j, z]) * part[z] for z in range(len(part)))
    return out


def from_cosines(f):
    n = len(f)
    even, out = [None] * (n // 2), [None] * n
    for z in range(n // 4):
        a = sum(float(QZ[j, z]) * f[j] for j in range(0, n, 4))
        b = sum(float(QZ[j, z]) * f[j] for j in range(2, n, 4))
        even[z], even[n // 2 - 1 - z] = a + b, a - b
    for z in range(n // 2):
        odd = sum(float(QZ[j, z]) * f[j] for j in range(1, n, 2))
        out[z], out[n - 1 - z] = even[z] + odd, even[z] - odd
    return out


def front_kernel(nn, nb, v_hbm, spacing, eig, modes_hbm, xw_hbm, edge_hl_hbm, edge_h_hbm, spec_h_hbm, spec_l_hbm,
                 back_h_hbm, back_l_hbm, mu_row, nu_lane, nu_row, mu_col, q_lane, turn_h, turn_l, unturn_h, unturn_l,
                 cos_b, ex_row, star_hbm, walls_hbm, pace_hbm, fh_hbm, got,
                 v, star, rim, zsend, zrecv, xsend, xrecv, s2send, s2recv, x0send, x0recv, x1send, x1recv,
                 load_sem, store_sem, z_ss, z_rs, x_ss, x_rs, s2_ss, s2_rs, x0_ss, x0_rs, x1_ss, x1_rs, e_ss, e_rs,
                 source, tiles, gz, gh, zl, zf, send, recv, back, s1, r1, s2, r2,
                 to_modes, xw, edge_hl, edge_h, spec_h, spec_l, back_h, back_l, const_sem, edge, t_high, t_low,
                 walls, pace, fh, out_sem):
    large = ((modes_hbm, to_modes), (xw_hbm, xw), (edge_hl_hbm, edge_hl), (edge_h_hbm, edge_h),
             (spec_h_hbm, spec_h), (spec_l_hbm, spec_l), (back_h_hbm, back_h), (back_l_hbm, back_l))
    me_n = lax.axis_index("narrow")
    me_b = lax.axis_index("wide")
    ring = nb // 4
    layer = me_b // ring
    spot = lax.rem(me_b, ring)
    up = (me_n, lax.rem(me_b + 1, nb))
    down = (me_n, lax.rem(me_b + nb - 1, nb))
    right = (lax.rem(me_n + 1, nn), me_b)
    left = (lax.rem(me_n + nn - 1, nn), me_b)

    loads = [pltpu.make_async_copy(v_hbm.at[c], v.at[c, pl.ds(LZ, ROWS)], load_sem.at[c]) for c in range(3)]
    for c in (2, 0, 1):
        loads[c].start()

    fetches = [pltpu.make_async_copy(h, m, const_sem.at[k]) for k, (h, m) in enumerate(large)]
    for cp in fetches:
        cp.start()
    barrier = pltpu.get_barrier_semaphore()
    narrow_peers = [(lax.rem(me_n + k, nn), me_b) for k in range(1, nn)]
    spot_peers = [(me_n, layer * ring + lax.rem(spot + k, ring)) for k in range(1, ring)]
    layer_peers = [(me_n, lax.rem(layer + k, 4) * ring + spot) for k in range(1, 4)]
    greeted = [up, down] + narrow_peers + spot_peers + layer_peers
    for peer in greeted:
        pl.semaphore_signal(barrier, inc=1, device_id=peer, device_id_type=MESH)

    zero = jnp.zeros((LZ, LX), jnp.float32)
    for c in range(3):
        v[c, pl.ds(0, LZ), :] = zero
        v[c, pl.ds(LZ + ROWS, LZ), :] = zero
        star[c, pl.ds(0, LZ), :] = zero
        star[c, pl.ds(LZ + ROWS, LZ), :] = zero
    each = NY // (nn * nb)
    me = me_n * nb + me_b
    which = lax.broadcasted_iota(jnp.int32, (8, LX), 0)
    values = jnp.zeros((8, LX), jnp.float32)
    for k in range(each):
        values = jnp.where(which == k, eig[k], values)
    tiles[pl.ds(pl.multiple_of(me * 8, 8), 8), :] = values
    pl.semaphore_wait(barrier, len(greeted))

    def share(peers, at, count, stage):
        for k, peer in enumerate(peers):
            pltpu.make_async_remote_copy(
                src_ref=tiles.at[pl.ds(pl.multiple_of(at * 8, 8), count * 8)], dst_ref=tiles.at[pl.ds(pl.multiple_of(at * 8, 8), count * 8)],
                send_sem=e_ss.at[stage], recv_sem=e_rs.at[stage], device_id=peer, device_id_type=MESH).start()

    def share_wait(peers, count, stage):
        n = len(peers) * count
        w = pltpu.make_async_remote_copy(
            src_ref=tiles.at[pl.ds(0, n * 8)], dst_ref=tiles.at[pl.ds(0, n * 8)],
            send_sem=e_ss.at[stage], recv_sem=e_rs.at[stage], device_id=peers[0], device_id_type=MESH)
        w.wait_send()
        w.wait_recv()

    def remote(src_ref, dst_ref, ss, rs, peer):
        return pltpu.make_async_remote_copy(src_ref=src_ref, dst_ref=dst_ref, send_sem=ss, recv_sem=rs,
                                            device_id=peer, device_id_type=MESH)

    lane = lax.broadcasted_iota(jnp.int32, (LZ, LX), 1)
    level = lax.broadcasted_iota(jnp.int32, (LZ, LX), 0)

    def pack(ref, c, out):
        def step(yy, carry):
            here, next_lane = lane == yy, lane == lax.rem(yy + 1, LX)
            result = []
            for g, (last, first) in enumerate(carry):
                plane = ref[c, pl.ds(pl.multiple_of(LZ + (g * LX + yy) * LZ, LZ), LZ), :]
                turned = pltpu.roll(plane, lax.rem(yy + 1, LX), 1)
                result.append((jnp.where(here, turned, last), jnp.where(next_lane, turned, first)))
            return tuple(result)
        ends = lax.fori_loop(0, LX, step, ((zero, zero),) * GROUPS, unroll=16)
        for g, (last, first) in enumerate(ends):
            out[0, g] = last
            out[1, g] = pltpu.roll(first, LX - 1, 1)

    share(spot_peers, me, 1, 0)
    def outward_z(c, side):
        return remote(zsend.at[side, c], zrecv.at[side, c], z_ss.at[side, c], z_rs.at[side, c], (up, down)[side])

    def outward_x(c, side):
        return remote(xsend.at[c, side], xrecv.at[side, c], x_ss.at[side, c], x_rs.at[side, c], (right, left)[side])

    def component(i, _):
        c = lax.rem(i + 2, 3)
        pltpu.make_async_copy(v_hbm.at[c], v.at[c, pl.ds(LZ, ROWS)], load_sem.at[c]).wait()
        pack(v, c, xsend.at[c])
        for side in range(2):
            outward_x(c, side).start()
        return 0

    def component_z(i, _):
        c = lax.rem(i + 2, 3)
        zsend[0, c] = v[c, pl.ds(LZ + LZ - 1, NY, stride=LZ), :]
        zsend[1, c] = v[c, pl.ds(LZ, NY, stride=LZ), :]
        for side in range(2):
            outward_z(c, side).start()
        return 0

    lax.fori_loop(0, 3, component, 0)
    lax.fori_loop(0, 3, component_z, 0)
    zcopies = [outward_z(c, side) for c in range(3) for side in range(2)]
    xcopies = [outward_x(c, side) for c in range(3) for side in range(2)]

    share_wait(spot_peers, 1, 0)
    share(layer_peers, me_n * nb + layer * ring, ring, 1)
    for cp in xcopies:
        cp.wait_recv()
    even = lax.rem(lane, 2) == 0

    def interleave(east, west):
        west = pltpu.roll(west, 1, 1)
        return jnp.where(even, east, west), jnp.where(even, west, east)

    for c in range(3):
        for g in range(GROUPS):
            rim[c, g, 0], rim[c, g, 1] = interleave(xrecv[1, c, g], xrecv[0, c, g])

    def predict_plane(y, odd):
        g = y // LX
        yy = lax.rem(y, LX)
        base = pl.multiple_of(LZ + y * LZ, LZ)
        s = spacing[y]
        centre = [v[c, pl.ds(base, LZ), :] for c in range(3)]
        a_e = 0.05 - 0.05 * centre[0]
        a_w = 0.05 + 0.05 * centre[0]
        a_n = jnp.where(level == LZ - 1, 0.0, 0.05 - 0.05 * centre[2])
        a_s = jnp.where(level == 0, 0.0, 0.05 + 0.05 * centre[2])
        curve = 0.05 * s * s
        slope = (0.05 * s) * centre[1]
        a_u = curve - slope
        a_l = curve + slope
        a_c = 0.8 - 2.0 * curve
        for c in range(3):
            f = centre[c]
            upper = v[c, pl.ds(base + LZ, LZ), :]
            lower = v[c, pl.ds(base - LZ, LZ), :]
            north = v[c, pl.ds(base + 1, LZ), :]
            south = v[c, pl.ds(base - 1, LZ), :]
            ends = pltpu.roll(rim[c, g, odd], LX - 1 - yy, 1)
            east = jnp.where(lane == LX - 1, ends, pltpu.roll(f, LX - 1, 1))
            west = jnp.where(lane == 0, ends, pltpu.roll(f, 1, 1))
            star[c, pl.ds(base, LZ), :] = (
                a_c * f + a_e * east + a_w * west + (a_n * north + a_s * south) + (a_u * upper + a_l * lower))

    def predict_pair(k, _):
        predict_plane(2 * k, 0)
        predict_plane(2 * k + 1, 1)
        return 0

    lax.fori_loop(0, NY // 2, predict_pair, 0, unroll=8)

    share_wait(layer_peers, ring, 1)
    share(narrow_peers, me_n * nb, nb, 2)
    pack(star, 0, x0send)
    x0copies = [remote(x0send.at[side], x0recv.at[side], x0_ss.at[side], x0_rs.at[side], peer)
                for side, peer in ((0, right), (1, left))]
    for cp in x0copies:
        cp.start()
    def pace_row(y, _):
        pace[pl.ds(y, 1), :] = jnp.full((1, LX), spacing[y], jnp.float32)
        return 0

    lax.fori_loop(0, NY, pace_row, 0, unroll=8)
    f32 = jnp.float32
    nd = nn * nb
    for cp in fetches:
        cp.wait()
    t_high[...], t_low[...] = split(to_modes[...])

    def diverge_plane(y, odd):
        g = y // LX
        yy = lax.rem(y, LX)
        base = pl.multiple_of(LZ + y * LZ, LZ)
        s = 5.0 * spacing[y]
        f = star[0, pl.ds(base, LZ), :]
        east = jnp.where(lane == LX - 1, 0.0, pltpu.roll(f, LX - 1, 1))
        west = jnp.where(lane == 0, 0.0, pltpu.roll(f, 1, 1))
        north = star[2, pl.ds(base + 1, LZ), :]
        south = star[2, pl.ds(base - 1, LZ), :]
        rise = star[1, pl.ds(base + LZ, LZ), :] - star[1, pl.ds(base - LZ, LZ), :]
        source[pl.ds(y, LZ, stride=NY), :] = 5.0 * ((east - west) + (north - south)) + s * rise

    def diverge_pair(k, _):
        diverge_plane(2 * k, 0)
        diverge_plane(2 * k + 1, 1)
        return 0

    lax.fori_loop(0, NY // 2, diverge_pair, 0, unroll=8)

    for cp in zcopies:
        cp.wait_recv()
    part = 96
    for c in (2, 0, 1):
        def mend(k, _, c=c):
            hi = LZ + LZ - 1 + k * part * LZ
            lo = LZ + k * part * LZ
            rows = pl.ds(pl.multiple_of(k * part, 8), part)
            top = star[c, pl.ds(hi, part, stride=LZ), :] + zrecv[1, c, rows, :] * (
                0.05 - 0.05 * v[2, pl.ds(hi, part, stride=LZ), :])
            low = star[c, pl.ds(lo, part, stride=LZ), :] + zrecv[0, c, rows, :] * (
                0.05 + 0.05 * v[2, pl.ds(lo, part, stride=LZ), :])
            if c == 2:
                near_top = pl.ds(pl.multiple_of((LZ - 2) * NY + k * part, 8), part)
                near_low = pl.ds(pl.multiple_of(NY + k * part, 8), part)
                source[near_top, :] = source[near_top, :] + 5.0 * (top - star[c, pl.ds(hi, part, stride=LZ), :])
                source[near_low, :] = source[near_low, :] - 5.0 * (low - star[c, pl.ds(lo, part, stride=LZ), :])
            star[c, pl.ds(hi, part, stride=LZ), :] = top
            star[c, pl.ds(lo, part, stride=LZ), :] = low
            if c == 2:
                s2send[0, rows, :] = top
                s2send[1, rows, :] = low
            return 0

        lax.fori_loop(0, NY // part, mend, 0)
        if c == 2:
            s2copies = [remote(s2send.at[side], s2recv.at[side], s2_ss.at[side], s2_rs.at[side], peer)
                        for side, peer in ((0, up), (1, down))]
            for cp in s2copies:
                cp.start()
        if c == 0:
            pack(star, 0, x1send)
            x1copies = [remote(x1send.at[side], x1recv.at[side], x1_ss.at[side], x1_rs.at[side], peer)
                        for side, peer in ((0, right), (1, left))]
            for cp in x1copies:
                cp.start()
    stores = [pltpu.make_async_copy(star.at[c, pl.ds(LZ, ROWS)], star_hbm.at[c], store_sem.at[c]) for c in range(3)]
    for cp in stores:
        cp.start()
    for cp in x0copies:
        cp.wait_recv()
    middle = (level > 0) & (level < LZ - 1)
    for g in range(GROUPS):
        x0recv[0, g] = jnp.where(middle, -5.0 * x0recv[0, g], 0.0)
        x0recv[1, g] = jnp.where(middle, 5.0 * x0recv[1, g], 0.0)
    ridge = lax.broadcasted_iota(jnp.int32, (LX, LX), 0)

    def whole(z):
        columns = [jnp.transpose(jnp.where(ridge == 0, x0recv[0, g, pl.ds(z, 1), :],
                                           jnp.where(ridge == LX - 1, x0recv[1, g, pl.ds(z, 1), :], 0.0)))
                   for g in range(GROUPS)]
        return source[pl.ds(pl.multiple_of(z * NY, LX), NY), :] + jnp.concatenate(columns, axis=0)

    def finish_outer():
        for cp in s2copies + x1copies:
            cp.wait_recv()
        square = lax.broadcasted_iota(jnp.int32, (LX, LX), 0)
        lanes = lax.broadcasted_iota(jnp.int32, (LX, LX), 1)
        for z, inner, sign, side in ((0, 1, 1.0, 0), (LZ - 1, LZ - 2, -1.0, 1)):
            def rows_of(g, _, z=z, inner=inner, sign=sign, side=side):
                first = LZ + z + g * (LX * LZ)
                rows = pl.ds(pl.multiple_of(g * LX, LX), LX)
                ends = jnp.transpose(jnp.where(square == 0, x1recv[0, g, z:z + 1, :], jnp.where(square == LX - 1, x1recv[1, g, z:z + 1, :], 0.0)))
                f = star[0, pl.ds(first, LX, stride=LZ), :]
                east = jnp.where(lanes == LX - 1, ends, pltpu.roll(f, LX - 1, 1))
                west = jnp.where(lanes == 0, ends, pltpu.roll(f, 1, 1))
                rise = star[1, pl.ds(first + LZ, LX, stride=LZ), :] - star[1, pl.ds(first - LZ, LX, stride=LZ), :]
                across = sign * (star[2, pl.ds(first + inner - z, LX, stride=LZ), :] - s2recv[side, rows, :])
                source[pl.ds(pl.multiple_of(z * NY + g * LX, LX), LX), :] = 5.0 * ((east - west) + across + pace[rows, :] * rise)
                return 0

            lax.fori_loop(0, GROUPS, rows_of, 0)

    def slabs(i, _):
        @pl.when(i == LZ // 2 - 2)
        def _():
            finish_outer()

        p = lax.rem(i + 1, LZ // 2)
        p = jnp.where(i == LZ // 2 - 2, LZ // 2 - 1, jnp.where(i == LZ // 2 - 1, 0, p))
        s_high, s_low = split(jnp.concatenate([whole(2 * p), whole(2 * p + 1)], axis=1))
        modal = mm(t_high[...], s_high) + mm(t_low[...], s_high) + mm(t_high[...], s_low)
        for k in range(2):
            high, low = split(modal[:, k * LX:(k + 1) * LX])
            both = mm(jnp.concatenate([high, low], axis=1), xw[...])
            gz[2 * p + k] = both[:, :LX] + both[:, LX:]
        return 0

    lax.fori_loop(0, LZ // 2, slabs, 0)
    share_wait(narrow_peers, nb, 2)
    each = NY // nd
    for k in range(each):
        walls[pl.ds(k, nd, stride=each), :] = tiles[pl.ds(k, nd, stride=8), :]

    def chunk(k, _):
        rows = pl.ds(pl.multiple_of(k * 8, 8), 8)
        f = to_cosines([gz[z, rows, :] for z in range(LZ)])
        base = walls[rows, :] + mu_row[...]
        sums = [None, None]
        for j in range(LZ):
            fh[j, rows, :] = f[j]
            g = f[j] * pl.reciprocal(base + float(NU[j]))
            gh[j, rows, :] = g
            term = float(QZL[j]) * g
            sums[j % 2] = term if sums[j % 2] is None else sums[j % 2] + term
        zl[rows, :] = sums[0] + sums[1]
        zf[rows, :] = sums[0] - sums[1]
        return 0

    lax.fori_loop(0, NY // 8, chunk, 0, unroll=2)
    edge[...] = jnp.zeros((NY, LX), f32)

    def ends_of(j, _):
        high, low = split(jnp.concatenate([gh[2 * j], gh[2 * j + 1]], axis=1))
        both = mm(high, edge_hl[j])
        edge[...] += both[:, :LX] + both[:, LX:] + mm(low, edge_h[j])
        return 0

    lax.fori_loop(0, LZ // 2, ends_of, 0)
    packed = edge[:nd]
    for r in range(R):
        rows = pl.ds(r * nd, nd)
        send[pl.ds(r, nd, stride=8), :] = zl[rows, :]
        send[pl.ds(R + r, nd, stride=8), :] = zf[rows, :]
        if r:
            packed = packed + pltpu.roll(edge[r * nd:(r + 1) * nd], SLOT * r, 1)
    send[pl.ds(2 * R, nd, stride=8), :] = packed
    send[pl.ds(2 * R + 1, nd, stride=8), :] = jnp.zeros((nd, LX), f32)

    def ship(src, dst, ss, rs):
        def go(k, _):
            d = me + k
            d = jnp.where(d >= nd, d - nd, d)
            pltpu.make_async_remote_copy(
                src_ref=src.at[pl.ds(pl.multiple_of(d * 8, 8), 8)], dst_ref=dst.at[pl.ds(pl.multiple_of(me * 8, 8), 8)],
                send_sem=ss, recv_sem=rs, device_id=d, device_id_type=pl.DeviceIdType.LOGICAL).start()
            return 0
        lax.fori_loop(1, nd, go, 0, unroll=8)
        mine = pl.ds(pl.multiple_of(me * 8, 8), 8)
        dst[mine, :] = src[mine, :]
        most = pl.ds(0, (nd - 1) * 8)
        return pltpu.make_async_remote_copy(src_ref=src.at[most], dst_ref=dst.at[most], send_sem=ss, recv_sem=rs,
                                            device_id=(me_n, me_b), device_id_type=MESH)

    out = ship(send, recv, s1, r1)
    results = [pltpu.make_async_copy(m, h, out_sem.at[k])
               for k, (m, h) in enumerate(((walls, walls_hbm), (pace, pace_hbm), (fh, fh_hbm)))]
    for cp in results:
        cp.start()

    own = [walls[pl.ds(r * nd + me, 1), :] for r in range(R)]
    lane = lax.broadcasted_iota(jnp.int32, (1, LX), 1)
    owner_lane = jnp.where(lane < SLOT, own[0], jnp.where(lane < 2 * SLOT, own[1], own[2]))
    rowid = lax.broadcasted_iota(jnp.int32, (LX, LX), 0)
    owner_row = jnp.where(rowid < SLOT, own[0], jnp.where(rowid < 2 * SLOT, own[1], own[2]))
    low_half = lax.rem(lane, SLOT) < LZ
    d_rows = pl.reciprocal(owner_row + nu_row[...] + mu_row[...])
    d_cols = pl.reciprocal(owner_lane + nu_lane[...] + mu_col[...])
    qxl, qxf = q_lane[0:1], q_lane[1:2]
    qzl = jnp.where(low_half, q_lane[2:3], 0.0)
    qzf = jnp.where(low_half, q_lane[3:4], 0.0)
    hll = jnp.sum(d_cols * q_lane[8:8 + LX], axis=0, keepdims=True)
    hlf = jnp.sum(d_cols * q_lane[8 + LX:8 + 2 * LX], axis=0, keepdims=True)
    l0, l1, l2 = (1.0 / (1 + 2 * hll - 2 * hlf), 1.0 / (1 + 2 * hll), 1.0 / (1 + 2 * hll + 2 * hlf))
    k0, k1, k2 = (0.25 * (l0 + 2 * l1 + l2), 0.25 * (l0 - l2), 0.25 * (l0 - 2 * l1 + l2))
    dr_h, dr_l = split(d_rows)
    dc_h, dc_l = split(d_cols)
    scale = []
    for r in range(R):
        gll = jnp.zeros_like(ex_row[...])
        glf = jnp.zeros_like(ex_row[...])
        base = jnp.concatenate([own[r]] * nn, axis=1) + ex_row[...]
        for j in range(LZ):
            g = 1.0 / (base + float(NU[j]))
            gll = gll + float(QZL[j] ** 2) * g
            glf = glf + float(QZL[j] * QZF[j]) * g
        scale.append(1.0 / (1 + 2 * gll - 2 * glf * cos_b[...]))
    scale = jnp.concatenate(scale, axis=0)

    def coupled(a):
        return [k0 * a[n] + k1 * (a[(n + 1) % nn] + a[(n - 1) % nn]) + k2 * a[(n + 2) % nn] for n in range(nn)]

    def ahead(a):
        return pltpu.roll(a, nb - 1, 0)

    def behind(a):
        return pltpu.roll(a, 1, 0)

    def blocks(a):
        return [a[n * nb:(n + 1) * nb] for n in range(nn)]

    out.wait_recv()
    x = blocks(recv[pl.ds(2 * R, nd, stride=8), :])
    t = coupled([jnp.where(low_half, x[n] - pltpu.roll(x[(n + 1) % nn], LX - LZ, 1), 0.0) for n in range(nn)])
    big = jnp.concatenate([qzl * t[n] - qzf * ahead(t[n]) for n in range(nn)], axis=0)
    lines = []
    for r in range(R):
        mine = (lane >= SLOT * r) & (lane < SLOT * (r + 1))
        td = blocks(mm3(jnp.where(mine, big, 0.0), dr_h, dr_l))
        last = blocks(recv[pl.ds(r, nd, stride=8), :])
        first = blocks(recv[pl.ds(R + r, nd, stride=8), :])
        lines.append(jnp.concatenate(
            [last[n] - ahead(first[n]) - (qxl * td[n] - qxf * td[(n - 1) % nn]) for n in range(nn)], axis=1))
    s = mm3(jnp.concatenate(lines, axis=0), spec_h[...], spec_l[...])
    s = jnp.concatenate([s, jnp.zeros((LX - R * nb, nn * LX), f32)], axis=0)
    s_h, s_l = split(s)
    s = mm(turn_h[...], s_h) + mm(turn_l[...], s_h) + mm(turn_h[...], s_l)
    s = jnp.concatenate([s[:R * nb] * scale, s[R * nb:]], axis=0)
    s_h, s_l = split(s)
    s = mm(unturn_h[...], s_h) + mm(unturn_l[...], s_h) + mm(unturn_h[...], s_l)
    y = mm3(s[:R * nb], back_h[...], back_l[...])
    zsum = jnp.zeros((nd, LX), f32)
    for r in range(R):
        yr = [y[r * nb:(r + 1) * nb, n * LX:(n + 1) * LX] for n in range(nn)]
        back[pl.ds(r, nd, stride=8), :] = jnp.concatenate(yr, axis=0)
        back[pl.ds(R + r, nd, stride=8), :] = jnp.concatenate([behind(a) for a in yr], axis=0)
        mine = (lane >= SLOT * r) & (lane < SLOT * (r + 1))
        ends = jnp.concatenate([qxl * yr[n] - qxf * yr[(n + 1) % nn] for n in range(nn)], axis=0)
        zsum = zsum + jnp.where(mine, mm3(ends, dc_h, dc_l), 0.0)
    zs = blocks(zsum)
    u = coupled([qzl * zs[n] - qzf * behind(zs[n]) for n in range(nn)])
    w = [jnp.where(low_half, t[n] - u[n], 0.0) for n in range(nn)]
    back[pl.ds(2 * R, nd, stride=8), :] = jnp.concatenate(
        [w[n] + pltpu.roll(w[(n - 1) % nn], LZ, 1) for n in range(nn)], axis=0)
    back[pl.ds(2 * R + 1, nd, stride=8), :] = jnp.zeros((nd, LX), f32)
    home = ship(back, got, s2, r2)
    out.wait_send()
    home.wait_recv()
    home.wait_send()
    for cp in zcopies + xcopies + s2copies + x0copies + x1copies:
        cp.wait_send()
    for cp in stores + results:
        cp.wait()


def front_part(velocity, inv_spacing, eigen_wall, to_modes):
    nn, nb = lax.axis_size("narrow"), lax.axis_size("wide")
    f32 = jnp.float32
    nd = nn * nb
    edge = np.zeros((LZ, LX, LX))
    for j in range(LZ):
        edge[j, :, j] = QXL
        edge[j, :, LZ + j] = QXF
    edge_h, edge_l = halves(edge.reshape(LZ // 2, 2 * LX, LX))
    slot = np.arange(LX) % LZ
    nu_lane = NU[slot][None]
    table, ex = fourier(nn * LX)
    spec = np.einsum("knx,ix->nik", table.reshape(-1, nn, LX), QX).reshape(nn * LX, nn * LX)
    turn, eb = fourier(nb)
    turn = np.kron(np.eye(LX // nb), turn)
    q_lane = np.zeros((8 + 2 * LX, LX))
    q_lane[0], q_lane[1], q_lane[2], q_lane[3] = QXL, QXF, QZL[slot], QZF[slot]
    q_lane[8:8 + LX] = (QXL ** 2)[:, None]
    q_lane[8 + LX:] = (QXL * QXF)[:, None]
    big = [paired(QX.T), np.concatenate([edge_h, edge_l], axis=2), edge_h, *halves(spec), *halves(spec.T)]
    small = [MU[None], nu_lane, np.broadcast_to(NU[slot][:, None], (LX, LX)), np.broadcast_to(MU[:, None], (LX, LX)), q_lane,
             *halves(turn), *halves(turn.T), np.broadcast_to(1 - eb[:, None] / 2, (nb, nn * LX)), ex[None]]
    consts = [jnp.asarray(a if a.dtype == ml_dtypes.bfloat16 else a.astype(np.float32)) for a in big + small]
    any_, vmem, smem = (pl.BlockSpec(memory_space=m) for m in (pl.ANY, pltpu.VMEM, pltpu.SMEM))
    dma = pltpu.SemaphoreType.DMA
    return pl.pallas_call(
        functools.partial(front_kernel, nn, nb),
        out_shape=(jax.ShapeDtypeStruct((3, ROWS, LX), f32), *[jax.ShapeDtypeStruct((NY, LX), f32)] * 2,
                   jax.ShapeDtypeStruct((LZ, NY, LX), f32), jax.ShapeDtypeStruct((nd * 8, LX), f32)),
        in_specs=[any_, smem, smem] + [any_] * (1 + len(big)) + [vmem] * len(small),
        out_specs=(any_, any_, any_, any_, vmem),
        scratch_shapes=[
            pltpu.VMEM((3, ROWS + 2 * LZ, LX), f32), pltpu.VMEM((3, ROWS + 2 * LZ, LX), f32), pltpu.VMEM((3, GROUPS, 2, LZ, LX), f32),
            pltpu.VMEM((2, 3, NY, LX), f32), pltpu.VMEM((2, 3, NY, LX), f32),
            pltpu.VMEM((3, 2, GROUPS, LZ, LX), f32), pltpu.VMEM((2, 3, GROUPS, LZ, LX), f32),
            pltpu.VMEM((2, NY, LX), f32), pltpu.VMEM((2, NY, LX), f32),
            *[pltpu.VMEM((2, GROUPS, LZ, LX), f32)] * 4,
            dma((3,)), dma((3,)), dma((2, 3)), dma((2, 3)), dma((2, 3)), dma((2, 3)),
            *[dma((2,))] * 6, dma((3,)), dma((3,)),
            pltpu.VMEM((LZ * NY, LX), f32), pltpu.VMEM((nd * 8, LX), f32),
            pltpu.VMEM((LZ, NY, LX), f32), pltpu.VMEM((LZ, NY, LX), f32), pltpu.VMEM((NY, LX), f32), pltpu.VMEM((NY, LX), f32),
            pltpu.VMEM((nd * 8, LX), f32), pltpu.VMEM((nd * 8, LX), f32), pltpu.VMEM((nd * 8, LX), f32),
            dma, dma, dma, dma,
            pltpu.VMEM((NY, NY), f32), *[pltpu.VMEM(a.shape, jnp.bfloat16) for a in big], dma((1 + len(big),)),
            pltpu.VMEM((NY, LX), f32), pltpu.VMEM((NY, NY), jnp.bfloat16), pltpu.VMEM((NY, NY), jnp.bfloat16),
            pltpu.VMEM((NY, LX), f32), pltpu.VMEM((NY, LX), f32), pltpu.VMEM((LZ, NY, LX), f32), dma((3,)),
        ],
        compiler_params=pltpu.CompilerParams(collective_id=0, has_side_effects=True, vmem_limit_bytes=60 * 1024 * 1024),
        name="predict_solve",
    )(velocity.reshape(3, ROWS, LX), inv_spacing, eigen_wall, to_modes, *consts)


def last_kernel(fh, got, walls, from_modes, spacing, star_hbm, mu_row, xw, side_x, side_z, out_hbm,
                star, ph, press, across, load_sem, store_sem):
    f32 = jnp.float32
    loads = [pltpu.make_async_copy(star_hbm.at[c], star.at[c], load_sem.at[c]) for c in range(3)]
    for cp in loads:
        cp.start()
    nd = got.shape[0] // 8
    lane = lax.broadcasted_iota(jnp.int32, (nd, LX), 1)
    rim = got[pl.ds(2 * R, nd, stride=8), :]
    cols = []
    for r in range(R):
        a = jnp.where(lane < SLOT, rim if r == 0 else pltpu.roll(rim, LX - SLOT * r, 1), 0.0)
        high = a.astype(jnp.bfloat16).astype(f32)
        low = a - high
        cols.append(high + pltpu.roll(low, SLOT, 1) + pltpu.roll(high, 2 * SLOT, 1))
    cols = jnp.concatenate(cols, axis=0).astype(jnp.bfloat16)
    yb = [got[pl.ds(r, nd, stride=8), :] for r in range(R)]
    ya = [got[pl.ds(R + r, nd, stride=8), :] for r in range(R)]
    for r in range(R):
        across[0, pl.ds(r * nd, nd), :] = yb[r]
        across[1, pl.ds(r * nd, nd), :] = ya[r]
    for j in range(LZ):
        ph[1 + j] = mm(cols, side_x[:, j * LX:(j + 1) * LX])

    def chunk(k, _):
        rows = pl.ds(pl.multiple_of(k * 8, 8), 8)
        b, a = across[0, rows, :], across[1, rows, :]
        jump = (b - a, b + a)
        base = walls[rows, :] + mu_row[...]
        f = [(float(QZL[j]) * jump[j % 2] + (ph[1 + j, rows, :] - fh[j, rows, :])) * pl.reciprocal(base + float(NU[j]))
             for j in range(LZ)]
        x = from_cosines(f)
        for z in range(LZ):
            ph[1 + z, rows, :] = x[z]
        ph[0, rows, :] = x[0] - a
        ph[LZ + 1, rows, :] = x[LZ - 1] + b
        return 0

    lax.fori_loop(0, NY // 8, chunk, 0)
    m_high, m_low = split(from_modes[...])

    def modes(a):
        high, low = split(a)
        return mm(m_high, high) + mm(m_low, high) + mm(m_high, low)

    zero = jnp.zeros((8, LX), f32)
    for z in range(0, LZ + 2, 2):
        pair = []
        for k in range(2):
            high, low = split(ph[z + k])
            both = mm(jnp.concatenate([high, low], axis=1), xw[...])
            pair.append(both[:, :LX] + both[:, LX:])
        both = modes(jnp.concatenate(pair, axis=1))
        for k in range(2):
            press[z + k, pl.ds(0, 8), :] = zero
            press[z + k, pl.ds(8, NY), :] = both[:, k * LX:(k + 1) * LX]
            press[z + k, pl.ds(8 + NY, 8), :] = zero
    across[0] = modes(mm(cols, side_z[...]))
    for cp in loads:
        cp.wait()
    part = 64
    lane = lax.broadcasted_iota(jnp.int32, (part, LX), 1)

    def store(k):
        rows = pl.ds(pl.multiple_of(k * part * LZ, 8), part * LZ)
        return [pltpu.make_async_copy(star.at[c, rows], out_hbm.at[c, rows], store_sem.at[c, k]) for c in range(3)]

    def correct(k, _):
        at = pl.multiple_of(k * part, part)
        rim = across[0, pl.ds(at, part), :]
        slope = 0.05 * spacing[pl.ds(at, part), :]
        for z in range(LZ):
            p = press[1 + z, pl.ds(at + 8, part), :]
            east = jnp.where(lane == LX - 1, p + rim[:, z:z + 1], pltpu.roll(p, LX - 1, 1))
            west = jnp.where(lane == 0, p - rim[:, LZ + z:LZ + z + 1], pltpu.roll(p, 1, 1))
            up = press[1 + z, pl.ds(at + 9, part), :]
            down = press[1 + z, pl.ds(at + 7, part), :]
            north = press[2 + z, pl.ds(at + 8, part), :]
            south = press[z, pl.ds(at + 8, part), :]
            rows = pl.ds(at * LZ + z, part, stride=LZ)
            star[0, rows, :] = star[0, rows, :] - 0.05 * (east - west)
            star[1, rows, :] = star[1, rows, :] - slope * (up - down)
            star[2, rows, :] = star[2, rows, :] - 0.05 * (north - south)
        for cp in store(k):
            cp.start()
        return 0

    lax.fori_loop(0, NY // part, correct, 0)

    def finish(k, _):
        for cp in store(k):
            cp.wait()
        return 0

    lax.fori_loop(0, NY // part, finish, 0)


def last_part(fh, got, walls, from_modes, spacing, star):
    f32 = jnp.float32
    side_x = np.zeros((SLOT, LZ, LX))
    side_z = np.zeros((SLOT, LX))
    for j in range(LZ):
        side_x[j, j] = QXL
        side_x[LZ + j, j] = -QXF
    side_z[:LZ, :LZ] = QZ
    side_z[LZ:, LZ:SLOT] = QZ

    def stacked(a):
        high, low = halves(a)
        return jnp.asarray(np.concatenate([high, high, low, np.zeros_like(low)], axis=0))

    consts = [jnp.asarray(MU[None].astype(np.float32)), jnp.asarray(paired(QX)),
              stacked(side_x.reshape(SLOT, LZ * LX)), stacked(side_z)]
    vmem, any_ = (pl.BlockSpec(memory_space=m) for m in (pltpu.VMEM, pl.ANY))
    parts = NY // 64
    return pl.pallas_call(
        last_kernel,
        out_shape=jax.ShapeDtypeStruct((3, ROWS, LX), f32),
        in_specs=[vmem] * 5 + [any_] + [vmem] * 4,
        out_specs=any_,
        scratch_shapes=[
            pltpu.VMEM((3, ROWS, LX), f32), pltpu.VMEM((LZ + 2, NY, LX), f32), pltpu.VMEM((LZ + 2, NY + 16, LX), f32),
            pltpu.VMEM((2, NY, LX), f32), pltpu.SemaphoreType.DMA((3,)), pltpu.SemaphoreType.DMA((3, parts)),
        ],
        compiler_params=pltpu.CompilerParams(vmem_limit_bytes=56 * 1024 * 1024),
        name="synthesis_correct",
    )(fh, got, walls, from_modes, spacing, star, *consts)


def shards(velocity, inv_spacing, eigen_wall, to_modes, from_modes):
    star, walls, spacing, fh, got = front_part(velocity, inv_spacing, eigen_wall, to_modes)
    return last_part(fh, got, walls, from_modes, spacing, star).reshape(3, NY, LZ, LX)


def solution(mesh):
    in_specs = (P(None, None, "wide", "narrow"), P(), P(("narrow", "wide")), P(), P())
    out_specs = P(None, None, "wide", "narrow")
    return jax.shard_map(shards, mesh=mesh, in_specs=in_specs, out_specs=out_specs, check_vma=False)
```

```python
import functools
import math

import jax
import jax.numpy as jnp
import ml_dtypes
import numpy as np
from jax import lax
from jax.experimental import pallas as pl
from jax.experimental.pallas import tpu as pltpu
from jax.sharding import PartitionSpec as P

MESH = pl.DeviceIdType.MESH
LZ = 16
LX = 128
NY = 384
ROWS = NY * LZ
GROUPS = NY // LX


def split(a):
    high = a.astype(jnp.bfloat16)
    return high, (a - high.astype(jnp.float32)).astype(jnp.bfloat16)


def mm(a, b):
    return jnp.dot(a, b, preferred_element_type=jnp.float32)


def mm3(a, b_high, b_low):
    high, low = split(a)
    return mm(high, b_high) + mm(low, b_high) + mm(high, b_low)


def cosines(n):
    j = np.arange(n)[:, None]
    z = np.arange(n)[None, :]
    q = np.cos(np.pi * j * (z + 0.5) / n) * np.where(j == 0, math.sqrt(1 / n), math.sqrt(2 / n))
    return q, 2 - 2 * np.cos(np.pi * np.arange(n) / n)


def fourier(n):
    r = np.arange(n)[:, None]
    c = np.arange(n)[None, :]
    mid = n // 2
    k = np.where(r <= mid, r, r - mid)
    phase = (k * c % n) * (2 * np.pi / n)
    waves = np.where(r <= mid, np.cos(phase), np.sin(phase))
    weight = np.where((r == 0) | (r == mid), math.sqrt(1 / n), math.sqrt(2 / n))
    return waves * weight, 2 - 2 * np.cos(2 * np.pi * k[:, 0] / n)


def halves(a):
    a = np.asarray(a, np.float32)
    high = a.astype(ml_dtypes.bfloat16)
    return high, (a - high.astype(np.float32)).astype(ml_dtypes.bfloat16)


def paired(a):
    high, low = halves(a)
    return np.block([[high, low], [high, np.zeros_like(low)]])


QZ, NU = cosines(LZ)
QX, MU = cosines(LX)
QZL, QZF = QZ[:, -1], QZ[:, 0]
QXL, QXF = QX[:, -1], QX[:, 0]
SLOT = 2 * LZ
R = 3


def to_cosines(x):
    n = len(x)
    out = [None] * n
    e = [x[z] + x[n - 1 - z] for z in range(n // 2)]
    o = [x[z] - x[n - 1 - z] for z in range(n // 2)]
    ee = [e[z] + e[n // 2 - 1 - z] for z in range(n // 4)]
    eo = [e[z] - e[n // 2 - 1 - z] for z in range(n // 4)]
    for j in range(n):
        part = o if j % 2 else (eo if j % 4 else ee)
        out[j] = sum(float(QZ[j, z]) * part[z] for z in range(len(part)))
    return out


def from_cosines(f):
    n = len(f)
    even, out = [None] * (n // 2), [None] * n
    for z in range(n // 4):
        a = sum(float(QZ[j, z]) * f[j] for j in range(0, n, 4))
        b = sum(float(QZ[j, z]) * f[j] for j in range(2, n, 4))
        even[z], even[n // 2 - 1 - z] = a + b, a - b
    for z in range(n // 2):
        odd = sum(float(QZ[j, z]) * f[j] for j in range(1, n, 2))
        out[z], out[n - 1 - z] = even[z] + odd, even[z] - odd
    return out


def front_kernel(nn, nb, v_hbm, spacing, eig, modes_hbm, xw_hbm, edge_hl_hbm, edge_h_hbm, spec_h_hbm, spec_l_hbm,
                 back_h_hbm, back_l_hbm, mu_row, nu_lane, nu_row, mu_col, q_lane, turn_h, turn_l, unturn_h, unturn_l,
                 cos_b, ex_row, star_hbm, walls_hbm, pace_hbm, fh_hbm, got,
                 v, star, rim, zsend, zrecv, xsend, xrecv, s2send, s2recv, x0send, x0recv, x1send, x1recv,
                 load_sem, store_sem, z_ss, z_rs, x_ss, x_rs, s2_ss, s2_rs, x0_ss, x0_rs, x1_ss, x1_rs, e_ss, e_rs,
                 source, tiles, gz, gh, zl, zf, send, recv, back, s1, r1, s2, r2,
                 to_modes, xw, edge_hl, edge_h, spec_h, spec_l, back_h, back_l, const_sem, edge, t_high, t_low,
                 walls, pace, fh, out_sem):
    large = ((modes_hbm, to_modes), (xw_hbm, xw), (edge_hl_hbm, edge_hl), (edge_h_hbm, edge_h),
             (spec_h_hbm, spec_h), (spec_l_hbm, spec_l), (back_h_hbm, back_h), (back_l_hbm, back_l))
    me_n = lax.axis_index("narrow")
    me_b = lax.axis_index("wide")
    ring = nb // 4
    layer = me_b // ring
    spot = lax.rem(me_b, ring)
    up = (me_n, lax.rem(me_b + 1, nb))
    down = (me_n, lax.rem(me_b + nb - 1, nb))
    right = (lax.rem(me_n + 1, nn), me_b)
    left = (lax.rem(me_n + nn - 1, nn), me_b)

    loads = [pltpu.make_async_copy(v_hbm.at[c], v.at[c, pl.ds(LZ, ROWS)], load_sem.at[c]) for c in range(3)]
    for c in (2, 0, 1):
        loads[c].start()

    fetches = [pltpu.make_async_copy(h, m, const_sem.at[k]) for k, (h, m) in enumerate(large)]
    for cp in fetches:
        cp.start()
    barrier = pltpu.get_barrier_semaphore()
    narrow_peers = [(lax.rem(me_n + k, nn), me_b) for k in range(1, nn)]
    spot_peers = [(me_n, layer * ring + lax.rem(spot + k, ring)) for k in range(1, ring)]
    layer_peers = [(me_n, lax.rem(layer + k, 4) * ring + spot) for k in range(1, 4)]
    greeted = [up, down] + narrow_peers + spot_peers + layer_peers
    for peer in greeted:
        pl.semaphore_signal(barrier, inc=1, device_id=peer, device_id_type=MESH)

    zero = jnp.zeros((LZ, LX), jnp.float32)
    for c in range(3):
        v[c, pl.ds(0, LZ), :] = zero
        v[c, pl.ds(LZ + ROWS, LZ), :] = zero
        star[c, pl.ds(0, LZ), :] = zero
        star[c, pl.ds(LZ + ROWS, LZ), :] = zero
    each = NY // (nn * nb)
    me = me_n * nb + me_b
    which = lax.broadcasted_iota(jnp.int32, (8, LX), 0)
    values = jnp.zeros((8, LX), jnp.float32)
    for k in range(each):
        values = jnp.where(which == k, eig[k], values)
    tiles[pl.ds(pl.multiple_of(me * 8, 8), 8), :] = values
    pl.semaphore_wait(barrier, len(greeted))

    def share(peers, at, count, stage):
        for k, peer in enumerate(peers):
            pltpu.make_async_remote_copy(
                src_ref=tiles.at[pl.ds(pl.multiple_of(at * 8, 8), count * 8)], dst_ref=tiles.at[pl.ds(pl.multiple_of(at * 8, 8), count * 8)],
                send_sem=e_ss.at[stage], recv_sem=e_rs.at[stage], device_id=peer, device_id_type=MESH).start()

    def share_wait(peers, count, stage):
        n = len(peers) * count
        w = pltpu.make_async_remote_copy(
            src_ref=tiles.at[pl.ds(0, n * 8)], dst_ref=tiles.at[pl.ds(0, n * 8)],
            send_sem=e_ss.at[stage], recv_sem=e_rs.at[stage], device_id=peers[0], device_id_type=MESH)
        w.wait_send()
        w.wait_recv()

    def remote(src_ref, dst_ref, ss, rs, peer):
        return pltpu.make_async_remote_copy(src_ref=src_ref, dst_ref=dst_ref, send_sem=ss, recv_sem=rs,
                                            device_id=peer, device_id_type=MESH)

    lane = lax.broadcasted_iota(jnp.int32, (LZ, LX), 1)
    level = lax.broadcasted_iota(jnp.int32, (LZ, LX), 0)

    def pack(ref, c, out):
        def step(yy, carry):
            here, next_lane = lane == yy, lane == lax.rem(yy + 1, LX)
            result = []
            for g, (last, first) in enumerate(carry):
                plane = ref[c, pl.ds(pl.multiple_of(LZ + (g * LX + yy) * LZ, LZ), LZ), :]
                turned = pltpu.roll(plane, lax.rem(yy + 1, LX), 1)
                result.append((jnp.where(here, turned, last), jnp.where(next_lane, turned, first)))
            return tuple(result)
        ends = lax.fori_loop(0, LX, step, ((zero, zero),) * GROUPS, unroll=16)
        for g, (last, first) in enumerate(ends):
            out[0, g] = last
            out[1, g] = pltpu.roll(first, LX - 1, 1)

    share(spot_peers, me, 1, 0)
    def outward_z(c, side):
        return remote(zsend.at[side, c], zrecv.at[side, c], z_ss.at[side, c], z_rs.at[side, c], (up, down)[side])

    def outward_x(c, side):
        return remote(xsend.at[c, side], xrecv.at[side, c], x_ss.at[side, c], x_rs.at[side, c], (right, left)[side])

    def component(i, _):
        c = lax.rem(i + 2, 3)
        pltpu.make_async_copy(v_hbm.at[c], v.at[c, pl.ds(LZ, ROWS)], load_sem.at[c]).wait()
        pack(v, c, xsend.at[c])
        for side in range(2):
            outward_x(c, side).start()
        return 0

    def component_z(i, _):
        c = lax.rem(i + 2, 3)
        zsend[0, c] = v[c, pl.ds(LZ + LZ - 1, NY, stride=LZ), :]
        zsend[1, c] = v[c, pl.ds(LZ, NY, stride=LZ), :]
        for side in range(2):
            outward_z(c, side).start()
        return 0

    lax.fori_loop(0, 3, component, 0)
    lax.fori_loop(0, 3, component_z, 0)
    zcopies = [outward_z(c, side) for c in range(3) for side in range(2)]
    xcopies = [outward_x(c, side) for c in range(3) for side in range(2)]

    share_wait(spot_peers, 1, 0)
    share(layer_peers, me_n * nb + layer * ring, ring, 1)
    for cp in xcopies:
        cp.wait_recv()
    even = lax.rem(lane, 2) == 0

    def interleave(east, west):
        west = pltpu.roll(west, 1, 1)
        return jnp.where(even, east, west), jnp.where(even, west, east)

    for c in range(3):
        for g in range(GROUPS):
            rim[c, g, 0], rim[c, g, 1] = interleave(xrecv[1, c, g], xrecv[0, c, g])

    def predict_plane(y, odd):
        g = y // LX
        yy = lax.rem(y, LX)
        base = pl.multiple_of(LZ + y * LZ, LZ)
        s = spacing[y]
        centre = [v[c, pl.ds(base, LZ), :] for c in range(3)]
        a_e = 0.05 - 0.05 * centre[0]
        a_w = 0.05 + 0.05 * centre[0]
        a_n = jnp.where(level == LZ - 1, 0.0, 0.05 - 0.05 * centre[2])
        a_s = jnp.where(level == 0, 0.0, 0.05 + 0.05 * centre[2])
        curve = 0.05 * s * s
        slope = (0.05 * s) * centre[1]
        a_u = curve - slope
        a_l = curve + slope
        a_c = 0.8 - 2.0 * curve
        for c in range(3):
            f = centre[c]
            upper = v[c, pl.ds(base + LZ, LZ), :]
            lower = v[c, pl.ds(base - LZ, LZ), :]
            north = v[c, pl.ds(base + 1, LZ), :]
            south = v[c, pl.ds(base - 1, LZ), :]
            ends = pltpu.roll(rim[c, g, odd], LX - 1 - yy, 1)
            east = jnp.where(lane == LX - 1, ends, pltpu.roll(f, LX - 1, 1))
            west = jnp.where(lane == 0, ends, pltpu.roll(f, 1, 1))
            star[c, pl.ds(base, LZ), :] = (
                a_c * f + a_e * east + a_w * west + (a_n * north + a_s * south) + (a_u * upper + a_l * lower))

    def predict_pair(k, _):
        predict_plane(2 * k, 0)
        predict_plane(2 * k + 1, 1)
        return 0

    lax.fori_loop(0, NY // 2, predict_pair, 0, unroll=12)

    share_wait(layer_peers, ring, 1)
    share(narrow_peers, me_n * nb, nb, 2)
    pack(star, 0, x0send)
    x0copies = [remote(x0send.at[side], x0recv.at[side], x0_ss.at[side], x0_rs.at[side], peer)
                for side, peer in ((0, right), (1, left))]
    for cp in x0copies:
        cp.start()
    def pace_row(y, _):
        pace[pl.ds(y, 1), :] = jnp.full((1, LX), spacing[y], jnp.float32)
        return 0

    lax.fori_loop(0, NY, pace_row, 0, unroll=8)
    f32 = jnp.float32
    nd = nn * nb
    for cp in fetches:
        cp.wait()
    t_high[...], t_low[...] = split(to_modes[...])

    def diverge_plane(y, odd):
        g = y // LX
        yy = lax.rem(y, LX)
        base = pl.multiple_of(LZ + y * LZ, LZ)
        s = 5.0 * spacing[y]
        f = star[0, pl.ds(base, LZ), :]
        east = jnp.where(lane == LX - 1, 0.0, pltpu.roll(f, LX - 1, 1))
        west = jnp.where(lane == 0, 0.0, pltpu.roll(f, 1, 1))
        north = star[2, pl.ds(base + 1, LZ), :]
        south = star[2, pl.ds(base - 1, LZ), :]
        rise = star[1, pl.ds(base + LZ, LZ), :] - star[1, pl.ds(base - LZ, LZ), :]
        source[pl.ds(y, LZ, stride=NY), :] = 5.0 * ((east - west) + (north - south)) + s * rise

    def diverge_pair(k, _):
        diverge_plane(2 * k, 0)
        diverge_plane(2 * k + 1, 1)
        return 0

    lax.fori_loop(0, NY // 2, diverge_pair, 0, unroll=16)

    for cp in zcopies:
        cp.wait_recv()
    part = 96
    for c in (2, 0, 1):
        def mend(k, _, c=c):
            hi = LZ + LZ - 1 + k * part * LZ
            lo = LZ + k * part * LZ
            rows = pl.ds(pl.multiple_of(k * part, 8), part)
            top = star[c, pl.ds(hi, part, stride=LZ), :] + zrecv[1, c, rows, :] * (
                0.05 - 0.05 * v[2, pl.ds(hi, part, stride=LZ), :])
            low = star[c, pl.ds(lo, part, stride=LZ), :] + zrecv[0, c, rows, :] * (
                0.05 + 0.05 * v[2, pl.ds(lo, part, stride=LZ), :])
            if c == 2:
                near_top = pl.ds(pl.multiple_of((LZ - 2) * NY + k * part, 8), part)
                near_low = pl.ds(pl.multiple_of(NY + k * part, 8), part)
                source[near_top, :] = source[near_top, :] + 5.0 * (top - star[c, pl.ds(hi, part, stride=LZ), :])
                source[near_low, :] = source[near_low, :] - 5.0 * (low - star[c, pl.ds(lo, part, stride=LZ), :])
            star[c, pl.ds(hi, part, stride=LZ), :] = top
            star[c, pl.ds(lo, part, stride=LZ), :] = low
            if c == 2:
                s2send[0, rows, :] = top
                s2send[1, rows, :] = low
            return 0

        lax.fori_loop(0, NY // part, mend, 0)
        if c == 2:
            s2copies = [remote(s2send.at[side], s2recv.at[side], s2_ss.at[side], s2_rs.at[side], peer)
                        for side, peer in ((0, up), (1, down))]
            for cp in s2copies:
                cp.start()
        if c == 0:
            pack(star, 0, x1send)
            x1copies = [remote(x1send.at[side], x1recv.at[side], x1_ss.at[side], x1_rs.at[side], peer)
                        for side, peer in ((0, right), (1, left))]
            for cp in x1copies:
                cp.start()
    stores = [pltpu.make_async_copy(star.at[c, pl.ds(LZ, ROWS)], star_hbm.at[c], store_sem.at[c]) for c in range(3)]
    for cp in stores:
        cp.start()
    for cp in x0copies:
        cp.wait_recv()
    middle = (level > 0) & (level < LZ - 1)
    for g in range(GROUPS):
        x0recv[0, g] = jnp.where(middle, -5.0 * x0recv[0, g], 0.0)
        x0recv[1, g] = jnp.where(middle, 5.0 * x0recv[1, g], 0.0)
    ridge = lax.broadcasted_iota(jnp.int32, (LX, LX), 0)

    def whole(z):
        columns = [jnp.transpose(jnp.where(ridge == 0, x0recv[0, g, pl.ds(z, 1), :],
                                           jnp.where(ridge == LX - 1, x0recv[1, g, pl.ds(z, 1), :], 0.0)))
                   for g in range(GROUPS)]
        return source[pl.ds(pl.multiple_of(z * NY, LX), NY), :] + jnp.concatenate(columns, axis=0)

    def finish_outer():
        for cp in s2copies + x1copies:
            cp.wait_recv()
        square = lax.broadcasted_iota(jnp.int32, (LX, LX), 0)
        lanes = lax.broadcasted_iota(jnp.int32, (LX, LX), 1)
        for z, inner, sign, side in ((0, 1, 1.0, 0), (LZ - 1, LZ - 2, -1.0, 1)):
            def rows_of(g, _, z=z, inner=inner, sign=sign, side=side):
                first = LZ + z + g * (LX * LZ)
                rows = pl.ds(pl.multiple_of(g * LX, LX), LX)
                ends = jnp.transpose(jnp.where(square == 0, x1recv[0, g, z:z + 1, :], jnp.where(square == LX - 1, x1recv[1, g, z:z + 1, :], 0.0)))
                f = star[0, pl.ds(first, LX, stride=LZ), :]
                east = jnp.where(lanes == LX - 1, ends, pltpu.roll(f, LX - 1, 1))
                west = jnp.where(lanes == 0, ends, pltpu.roll(f, 1, 1))
                rise = star[1, pl.ds(first + LZ, LX, stride=LZ), :] - star[1, pl.ds(first - LZ, LX, stride=LZ), :]
                across = sign * (star[2, pl.ds(first + inner - z, LX, stride=LZ), :] - s2recv[side, rows, :])
                source[pl.ds(pl.multiple_of(z * NY + g * LX, LX), LX), :] = 5.0 * ((east - west) + across + pace[rows, :] * rise)
                return 0

            lax.fori_loop(0, GROUPS, rows_of, 0)

    def slabs(i, _):
        @pl.when(i == LZ // 2 - 2)
        def _():
            finish_outer()

        p = lax.rem(i + 1, LZ // 2)
        p = jnp.where(i == LZ // 2 - 2, LZ // 2 - 1, jnp.where(i == LZ // 2 - 1, 0, p))
        s_high, s_low = split(jnp.concatenate([whole(2 * p), whole(2 * p + 1)], axis=1))
        modal = mm(t_high[...], s_high) + mm(t_low[...], s_high) + mm(t_high[...], s_low)
        for k in range(2):
            high, low = split(modal[:, k * LX:(k + 1) * LX])
            both = mm(jnp.concatenate([high, low], axis=1), xw[...])
            gz[2 * p + k] = both[:, :LX] + both[:, LX:]
        return 0

    lax.fori_loop(0, LZ // 2, slabs, 0)
    share_wait(narrow_peers, nb, 2)
    each = NY // nd
    for k in range(each):
        walls[pl.ds(k, nd, stride=each), :] = tiles[pl.ds(k, nd, stride=8), :]

    def chunk(k, _):
        rows = pl.ds(pl.multiple_of(k * 8, 8), 8)
        f = to_cosines([gz[z, rows, :] for z in range(LZ)])
        base = walls[rows, :] + mu_row[...]
        sums = [None, None]
        for j in range(LZ):
            fh[j, rows, :] = f[j]
            g = f[j] * pl.reciprocal(base + float(NU[j]))
            gh[j, rows, :] = g
            term = float(QZL[j]) * g
            sums[j % 2] = term if sums[j % 2] is None else sums[j % 2] + term
        zl[rows, :] = sums[0] + sums[1]
        zf[rows, :] = sums[0] - sums[1]
        return 0

    lax.fori_loop(0, NY // 8, chunk, 0, unroll=2)
    edge[...] = jnp.zeros((NY, LX), f32)

    def ends_of(j, _):
        high, low = split(jnp.concatenate([gh[2 * j], gh[2 * j + 1]], axis=1))
        both = mm(high, edge_hl[j])
        edge[...] += both[:, :LX] + both[:, LX:] + mm(low, edge_h[j])
        return 0

    lax.fori_loop(0, LZ // 2, ends_of, 0)
    packed = edge[:nd]
    for r in range(R):
        rows = pl.ds(r * nd, nd)
        send[pl.ds(r, nd, stride=8), :] = zl[rows, :]
        send[pl.ds(R + r, nd, stride=8), :] = zf[rows, :]
        if r:
            packed = packed + pltpu.roll(edge[r * nd:(r + 1) * nd], SLOT * r, 1)
    send[pl.ds(2 * R, nd, stride=8), :] = packed
    send[pl.ds(2 * R + 1, nd, stride=8), :] = jnp.zeros((nd, LX), f32)

    def ship(src, dst, ss, rs):
        def go(k, _):
            d = me + k
            d = jnp.where(d >= nd, d - nd, d)
            pltpu.make_async_remote_copy(
                src_ref=src.at[pl.ds(pl.multiple_of(d * 8, 8), 8)], dst_ref=dst.at[pl.ds(pl.multiple_of(me * 8, 8), 8)],
                send_sem=ss, recv_sem=rs, device_id=d, device_id_type=pl.DeviceIdType.LOGICAL).start()
            return 0
        lax.fori_loop(1, nd, go, 0, unroll=8)
        mine = pl.ds(pl.multiple_of(me * 8, 8), 8)
        dst[mine, :] = src[mine, :]
        most = pl.ds(0, (nd - 1) * 8)
        return pltpu.make_async_remote_copy(src_ref=src.at[most], dst_ref=dst.at[most], send_sem=ss, recv_sem=rs,
                                            device_id=(me_n, me_b), device_id_type=MESH)

    out = ship(send, recv, s1, r1)
    results = [pltpu.make_async_copy(m, h, out_sem.at[k])
               for k, (m, h) in enumerate(((walls, walls_hbm), (pace, pace_hbm), (fh, fh_hbm)))]
    for cp in results:
        cp.start()

    own = [walls[pl.ds(r * nd + me, 1), :] for r in range(R)]
    lane = lax.broadcasted_iota(jnp.int32, (1, LX), 1)
    owner_lane = jnp.where(lane < SLOT, own[0], jnp.where(lane < 2 * SLOT, own[1], own[2]))
    rowid = lax.broadcasted_iota(jnp.int32, (LX, LX), 0)
    owner_row = jnp.where(rowid < SLOT, own[0], jnp.where(rowid < 2 * SLOT, own[1], own[2]))
    low_half = lax.rem(lane, SLOT) < LZ
    d_rows = pl.reciprocal(owner_row + nu_row[...] + mu_row[...])
    d_cols = pl.reciprocal(owner_lane + nu_lane[...] + mu_col[...])
    qxl, qxf = q_lane[0:1], q_lane[1:2]
    qzl = jnp.where(low_half, q_lane[2:3], 0.0)
    qzf = jnp.where(low_half, q_lane[3:4], 0.0)
    hll = jnp.sum(d_cols * q_lane[8:8 + LX], axis=0, keepdims=True)
    hlf = jnp.sum(d_cols * q_lane[8 + LX:8 + 2 * LX], axis=0, keepdims=True)
    l0, l1, l2 = (1.0 / (1 + 2 * hll - 2 * hlf), 1.0 / (1 + 2 * hll), 1.0 / (1 + 2 * hll + 2 * hlf))
    k0, k1, k2 = (0.25 * (l0 + 2 * l1 + l2), 0.25 * (l0 - l2), 0.25 * (l0 - 2 * l1 + l2))
    dr_h, dr_l = split(d_rows)
    dc_h, dc_l = split(d_cols)
    scale = []
    for r in range(R):
        gll = jnp.zeros_like(ex_row[...])
        glf = jnp.zeros_like(ex_row[...])
        base = jnp.concatenate([own[r]] * nn, axis=1) + ex_row[...]
        for j in range(LZ):
            g = 1.0 / (base + float(NU[j]))
            gll = gll + float(QZL[j] ** 2) * g
            glf = glf + float(QZL[j] * QZF[j]) * g
        scale.append(1.0 / (1 + 2 * gll - 2 * glf * cos_b[...]))
    scale = jnp.concatenate(scale, axis=0)

    def coupled(a):
        return [k0 * a[n] + k1 * (a[(n + 1) % nn] + a[(n - 1) % nn]) + k2 * a[(n + 2) % nn] for n in range(nn)]

    def ahead(a):
        return pltpu.roll(a, nb - 1, 0)

    def behind(a):
        return pltpu.roll(a, 1, 0)

    def blocks(a):
        return [a[n * nb:(n + 1) * nb] for n in range(nn)]

    out.wait_recv()
    x = blocks(recv[pl.ds(2 * R, nd, stride=8), :])
    t = coupled([jnp.where(low_half, x[n] - pltpu.roll(x[(n + 1) % nn], LX - LZ, 1), 0.0) for n in range(nn)])
    big = jnp.concatenate([qzl * t[n] - qzf * ahead(t[n]) for n in range(nn)], axis=0)
    lines = []
    for r in range(R):
        mine = (lane >= SLOT * r) & (lane < SLOT * (r + 1))
        td = blocks(mm3(jnp.where(mine, big, 0.0), dr_h, dr_l))
        last = blocks(recv[pl.ds(r, nd, stride=8), :])
        first = blocks(recv[pl.ds(R + r, nd, stride=8), :])
        lines.append(jnp.concatenate(
            [last[n] - ahead(first[n]) - (qxl * td[n] - qxf * td[(n - 1) % nn]) for n in range(nn)], axis=1))
    s = mm3(jnp.concatenate(lines, axis=0), spec_h[...], spec_l[...])
    s = jnp.concatenate([s, jnp.zeros((LX - R * nb, nn * LX), f32)], axis=0)
    s_h, s_l = split(s)
    s = mm(turn_h[...], s_h) + mm(turn_l[...], s_h) + mm(turn_h[...], s_l)
    s = jnp.concatenate([s[:R * nb] * scale, s[R * nb:]], axis=0)
    s_h, s_l = split(s)
    s = mm(unturn_h[...], s_h) + mm(unturn_l[...], s_h) + mm(unturn_h[...], s_l)
    y = mm3(s[:R * nb], back_h[...], back_l[...])
    zsum = jnp.zeros((nd, LX), f32)
    for r in range(R):
        yr = [y[r * nb:(r + 1) * nb, n * LX:(n + 1) * LX] for n in range(nn)]
        back[pl.ds(r, nd, stride=8), :] = jnp.concatenate(yr, axis=0)
        back[pl.ds(R + r, nd, stride=8), :] = jnp.concatenate([behind(a) for a in yr], axis=0)
        mine = (lane >= SLOT * r) & (lane < SLOT * (r + 1))
        ends = jnp.concatenate([qxl * yr[n] - qxf * yr[(n + 1) % nn] for n in range(nn)], axis=0)
        zsum = zsum + jnp.where(mine, mm3(ends, dc_h, dc_l), 0.0)
    zs = blocks(zsum)
    u = coupled([qzl * zs[n] - qzf * behind(zs[n]) for n in range(nn)])
    w = [jnp.where(low_half, t[n] - u[n], 0.0) for n in range(nn)]
    back[pl.ds(2 * R, nd, stride=8), :] = jnp.concatenate(
        [w[n] + pltpu.roll(w[(n - 1) % nn], LZ, 1) for n in range(nn)], axis=0)
    back[pl.ds(2 * R + 1, nd, stride=8), :] = jnp.zeros((nd, LX), f32)
    home = ship(back, got, s2, r2)
    out.wait_send()
    home.wait_recv()
    home.wait_send()
    for cp in zcopies + xcopies + s2copies + x0copies + x1copies:
        cp.wait_send()
    for cp in stores + results:
        cp.wait()


def front_part(velocity, inv_spacing, eigen_wall, to_modes):
    nn, nb = lax.axis_size("narrow"), lax.axis_size("wide")
    f32 = jnp.float32
    nd = nn * nb
    edge = np.zeros((LZ, LX, LX))
    for j in range(LZ):
        edge[j, :, j] = QXL
        edge[j, :, LZ + j] = QXF
    edge_h, edge_l = halves(edge.reshape(LZ // 2, 2 * LX, LX))
    slot = np.arange(LX) % LZ
    nu_lane = NU[slot][None]
    table, ex = fourier(nn * LX)
    spec = np.einsum("knx,ix->nik", table.reshape(-1, nn, LX), QX).reshape(nn * LX, nn * LX)
    turn, eb = fourier(nb)
    turn = np.kron(np.eye(LX // nb), turn)
    q_lane = np.zeros((8 + 2 * LX, LX))
    q_lane[0], q_lane[1], q_lane[2], q_lane[3] = QXL, QXF, QZL[slot], QZF[slot]
    q_lane[8:8 + LX] = (QXL ** 2)[:, None]
    q_lane[8 + LX:] = (QXL * QXF)[:, None]
    big = [paired(QX.T), np.concatenate([edge_h, edge_l], axis=2), edge_h, *halves(spec), *halves(spec.T)]
    small = [MU[None], nu_lane, np.broadcast_to(NU[slot][:, None], (LX, LX)), np.broadcast_to(MU[:, None], (LX, LX)), q_lane,
             *halves(turn), *halves(turn.T), np.broadcast_to(1 - eb[:, None] / 2, (nb, nn * LX)), ex[None]]
    consts = [jnp.asarray(a if a.dtype == ml_dtypes.bfloat16 else a.astype(np.float32)) for a in big + small]
    any_, vmem, smem = (pl.BlockSpec(memory_space=m) for m in (pl.ANY, pltpu.VMEM, pltpu.SMEM))
    dma = pltpu.SemaphoreType.DMA
    return pl.pallas_call(
        functools.partial(front_kernel, nn, nb),
        out_shape=(jax.ShapeDtypeStruct((3, ROWS, LX), f32), *[jax.ShapeDtypeStruct((NY, LX), f32)] * 2,
                   jax.ShapeDtypeStruct((LZ, NY, LX), f32), jax.ShapeDtypeStruct((nd * 8, LX), f32)),
        in_specs=[any_, smem, smem] + [any_] * (1 + len(big)) + [vmem] * len(small),
        out_specs=(any_, any_, any_, any_, vmem),
        scratch_shapes=[
            pltpu.VMEM((3, ROWS + 2 * LZ, LX), f32), pltpu.VMEM((3, ROWS + 2 * LZ, LX), f32), pltpu.VMEM((3, GROUPS, 2, LZ, LX), f32),
            pltpu.VMEM((2, 3, NY, LX), f32), pltpu.VMEM((2, 3, NY, LX), f32),
            pltpu.VMEM((3, 2, GROUPS, LZ, LX), f32), pltpu.VMEM((2, 3, GROUPS, LZ, LX), f32),
            pltpu.VMEM((2, NY, LX), f32), pltpu.VMEM((2, NY, LX), f32),
            *[pltpu.VMEM((2, GROUPS, LZ, LX), f32)] * 4,
            dma((3,)), dma((3,)), dma((2, 3)), dma((2, 3)), dma((2, 3)), dma((2, 3)),
            *[dma((2,))] * 6, dma((3,)), dma((3,)),
            pltpu.VMEM((LZ * NY, LX), f32), pltpu.VMEM((nd * 8, LX), f32),
            pltpu.VMEM((LZ, NY, LX), f32), pltpu.VMEM((LZ, NY, LX), f32), pltpu.VMEM((NY, LX), f32), pltpu.VMEM((NY, LX), f32),
            pltpu.VMEM((nd * 8, LX), f32), pltpu.VMEM((nd * 8, LX), f32), pltpu.VMEM((nd * 8, LX), f32),
            dma, dma, dma, dma,
            pltpu.VMEM((NY, NY), f32), *[pltpu.VMEM(a.shape, jnp.bfloat16) for a in big], dma((1 + len(big),)),
            pltpu.VMEM((NY, LX), f32), pltpu.VMEM((NY, NY), jnp.bfloat16), pltpu.VMEM((NY, NY), jnp.bfloat16),
            pltpu.VMEM((NY, LX), f32), pltpu.VMEM((NY, LX), f32), pltpu.VMEM((LZ, NY, LX), f32), dma((3,)),
        ],
        compiler_params=pltpu.CompilerParams(collective_id=0, has_side_effects=True, vmem_limit_bytes=60 * 1024 * 1024),
        name="predict_solve",
    )(velocity.reshape(3, ROWS, LX), inv_spacing, eigen_wall, to_modes, *consts)


def last_kernel(fh, got, walls, from_modes, spacing, star_hbm, mu_row, xw, side_x, side_z, out_hbm,
                star, ph, press, across, load_sem, store_sem):
    f32 = jnp.float32
    loads = [pltpu.make_async_copy(star_hbm.at[c], star.at[c], load_sem.at[c]) for c in range(3)]
    for cp in loads:
        cp.start()
    nd = got.shape[0] // 8
    lane = lax.broadcasted_iota(jnp.int32, (nd, LX), 1)
    rim = got[pl.ds(2 * R, nd, stride=8), :]
    cols = []
    for r in range(R):
        a = jnp.where(lane < SLOT, rim if r == 0 else pltpu.roll(rim, LX - SLOT * r, 1), 0.0)
        high = a.astype(jnp.bfloat16).astype(f32)
        low = a - high
        cols.append(high + pltpu.roll(low, SLOT, 1) + pltpu.roll(high, 2 * SLOT, 1))
    cols = jnp.concatenate(cols, axis=0).astype(jnp.bfloat16)
    yb = [got[pl.ds(r, nd, stride=8), :] for r in range(R)]
    ya = [got[pl.ds(R + r, nd, stride=8), :] for r in range(R)]
    for r in range(R):
        across[0, pl.ds(r * nd, nd), :] = yb[r]
        across[1, pl.ds(r * nd, nd), :] = ya[r]
    for j in range(LZ):
        ph[1 + j] = mm(cols, side_x[:, j * LX:(j + 1) * LX])

    def chunk(k, _):
        rows = pl.ds(pl.multiple_of(k * 8, 8), 8)
        b, a = across[0, rows, :], across[1, rows, :]
        jump = (b - a, b + a)
        base = walls[rows, :] + mu_row[...]
        f = [(float(QZL[j]) * jump[j % 2] + (ph[1 + j, rows, :] - fh[j, rows, :])) * pl.reciprocal(base + float(NU[j]))
             for j in range(LZ)]
        x = from_cosines(f)
        for z in range(LZ):
            ph[1 + z, rows, :] = x[z]
        ph[0, rows, :] = x[0] - a
        ph[LZ + 1, rows, :] = x[LZ - 1] + b
        return 0

    lax.fori_loop(0, NY // 8, chunk, 0)
    m_high, m_low = split(from_modes[...])

    def modes(a):
        high, low = split(a)
        return mm(m_high, high) + mm(m_low, high) + mm(m_high, low)

    zero = jnp.zeros((8, LX), f32)
    for z in range(0, LZ + 2, 2):
        pair = []
        for k in range(2):
            high, low = split(ph[z + k])
            both = mm(jnp.concatenate([high, low], axis=1), xw[...])
            pair.append(both[:, :LX] + both[:, LX:])
        both = modes(jnp.concatenate(pair, axis=1))
        for k in range(2):
            press[z + k, pl.ds(0, 8), :] = zero
            press[z + k, pl.ds(8, NY), :] = both[:, k * LX:(k + 1) * LX]
            press[z + k, pl.ds(8 + NY, 8), :] = zero
    across[0] = modes(mm(cols, side_z[...]))
    for cp in loads:
        cp.wait()
    part = 64
    lane = lax.broadcasted_iota(jnp.int32, (part, LX), 1)

    def store(k):
        rows = pl.ds(pl.multiple_of(k * part * LZ, 8), part * LZ)
        return [pltpu.make_async_copy(star.at[c, rows], out_hbm.at[c, rows], store_sem.at[c, k]) for c in range(3)]

    def correct(k, _):
        at = pl.multiple_of(k * part, part)
        rim = across[0, pl.ds(at, part), :]
        slope = 0.05 * spacing[pl.ds(at, part), :]
        for z in range(LZ):
            p = press[1 + z, pl.ds(at + 8, part), :]
            east = jnp.where(lane == LX - 1, p + rim[:, z:z + 1], pltpu.roll(p, LX - 1, 1))
            west = jnp.where(lane == 0, p - rim[:, LZ + z:LZ + z + 1], pltpu.roll(p, 1, 1))
            up = press[1 + z, pl.ds(at + 9, part), :]
            down = press[1 + z, pl.ds(at + 7, part), :]
            north = press[2 + z, pl.ds(at + 8, part), :]
            south = press[z, pl.ds(at + 8, part), :]
            rows = pl.ds(at * LZ + z, part, stride=LZ)
            star[0, rows, :] = star[0, rows, :] - 0.05 * (east - west)
            star[1, rows, :] = star[1, rows, :] - slope * (up - down)
            star[2, rows, :] = star[2, rows, :] - 0.05 * (north - south)
        for cp in store(k):
            cp.start()
        return 0

    lax.fori_loop(0, NY // part, correct, 0)

    def finish(k, _):
        for cp in store(k):
            cp.wait()
        return 0

    lax.fori_loop(0, NY // part, finish, 0)


def last_part(fh, got, walls, from_modes, spacing, star):
    f32 = jnp.float32
    side_x = np.zeros((SLOT, LZ, LX))
    side_z = np.zeros((SLOT, LX))
    for j in range(LZ):
        side_x[j, j] = QXL
        side_x[LZ + j, j] = -QXF
    side_z[:LZ, :LZ] = QZ
    side_z[LZ:, LZ:SLOT] = QZ

    def stacked(a):
        high, low = halves(a)
        return jnp.asarray(np.concatenate([high, high, low, np.zeros_like(low)], axis=0))

    consts = [jnp.asarray(MU[None].astype(np.float32)), jnp.asarray(paired(QX)),
              stacked(side_x.reshape(SLOT, LZ * LX)), stacked(side_z)]
    vmem, any_ = (pl.BlockSpec(memory_space=m) for m in (pltpu.VMEM, pl.ANY))
    parts = NY // 64
    return pl.pallas_call(
        last_kernel,
        out_shape=jax.ShapeDtypeStruct((3, ROWS, LX), f32),
        in_specs=[vmem] * 5 + [any_] + [vmem] * 4,
        out_specs=any_,
        scratch_shapes=[
            pltpu.VMEM((3, ROWS, LX), f32), pltpu.VMEM((LZ + 2, NY, LX), f32), pltpu.VMEM((LZ + 2, NY + 16, LX), f32),
            pltpu.VMEM((2, NY, LX), f32), pltpu.SemaphoreType.DMA((3,)), pltpu.SemaphoreType.DMA((3, parts)),
        ],
        compiler_params=pltpu.CompilerParams(vmem_limit_bytes=56 * 1024 * 1024),
        name="synthesis_correct",
    )(fh, got, walls, from_modes, spacing, star, *consts)


def shards(velocity, inv_spacing, eigen_wall, to_modes, from_modes):
    star, walls, spacing, fh, got = front_part(velocity, inv_spacing, eigen_wall, to_modes)
    return last_part(fh, got, walls, from_modes, spacing, star).reshape(3, NY, LZ, LX)


def solution(mesh):
    in_specs = (P(None, None, "wide", "narrow"), P(), P(("narrow", "wide")), P(), P())
    out_specs = P(None, None, "wide", "narrow")
    return jax.shard_map(shards, mesh=mesh, in_specs=in_specs, out_specs=out_specs, check_vma=False)
```
